256 devices in a mesh: leaf: 32 (over z, x), agg: 2 (over core), probe: 4 (over y).
Axes of the slice: x: 4, y: 4, z: 8, core: 2. Of those that a mesh axis runs over, the one named last changes fastest.
Arguments:
- probes: float32 [4, 192, 8192], P('probe', None, ('leaf', 'agg')), may hold values from -16 to 16
- viscosity: float32 [192, 8192], P(None, ('leaf', 'agg')), may hold values from 0.1 to 10
- friction: float32 [192, 8192], P(None, ('leaf', 'agg')), may hold values from 0.05 to 1
- sensitivity: float32 [192, 8192], P(None, ('leaf', 'agg')), may hold values from 0.5 to 3
- misfit_weight: float32 [192, 8192], P(None, ('leaf', 'agg')), may hold values from 1 to 10
- grad_ref: float32 [192, 192], replicated, may hold values from -2 to 3, as said below
- trace_ref: float32 [192, 192], replicated, may hold values from -2 to 3
- coarse_modes: float32 [192, 128], replicated, may hold values from -0.4375 to 0.4375
- coarse_inv: float32 [512, 128, 128], P(('leaf', 'agg')), may hold values from -1 to 5, as said below
- peer_slots: int32 [64, 64, 16], P(('leaf', 'agg')), may hold values from -1 to 127, as said below
- local_pairs: int32 [2, 8192], P(None, ('leaf', 'agg')), may hold values from 0 to 127, as said below
- elem_agg: int32 [8192], P(('leaf', 'agg')), may hold values from 0 to 15
Outputs:
- incr_velocity: float32 [4, 192, 8192], P('probe', None, ('leaf', 'agg'))
- hess_action: float32 [4, 192, 8192], P('probe', None, ('leaf', 'agg'))
- trace_est: float32 [], replicated
The draws below stay inside these ranges and needn't reach their ends.
Inputs may be any that keep to these rules, and one draw needn't show every extreme that they name: `grad_ref`: nonsingular. `coarse_inv`: each block is symmetric positive definite. peer_slots[P, Q, s] >= 0 exactly when peer_slots[Q, P, s] >= 0; the filled slots of a pair come first; no slot of a pair P, P is filled; the partitions are blocks of a three-dimensional grid and only blocks that touch by a face, edge or corner share slots, so a partition has at most 26 partners; some pair of partitions fills all 16 slots. `local_pairs`: the two elements of a pair differ.
All inputs are finite; a program needn't handle non-finite values.
Results may differ from the reference program's by a relative error of at most 0.0003.
Values sent between devices are 32-bit elements; how exact they have to be, the bound alone decides.
A program may use at most 64 MiB of HBM per device.

```python
import math
import jax
import jax.numpy as jnp
from jax import lax

NDOF = 192
CW = 128
E_DEV = 128
AGG_DEV = 8
CAP = 16
ITERS = 2
SWEEPS = 3
NPART = 64
NE = 8192
NAGG = 512
GROUP_AGG = 16
NLP = 8192
PROBES = 4
N_LEAF = 32
N_AGG = 2


def draw_probes(key, part):
    subkey = jax.random.fold_in(key, 11)
    fraction = jnp.arange(NE, dtype=jnp.float32) / NE
    base = jnp.clip(jax.random.normal(subkey, (PROBES, NDOF, NE), jnp.float32), -4.0, 4.0)
    profile = jnp.exp(math.log(3.0) * fraction)
    return base * profile[None, None, :]


def near_identity(noise, factor):
    return factor * (jnp.eye(NDOF, dtype=jnp.float32) + 0.4 * noise / math.sqrt(NDOF))


def draw_grad_ref(key, part):
    subkey = jax.random.fold_in(key, 21)
    noise = jnp.clip(jax.random.normal(subkey, (NDOF, NDOF), jnp.float32), -4.0, 4.0)
    return near_identity(noise, 1.0)


def draw_trace_ref(key, part):
    subkey = jax.random.fold_in(key, 22)
    noise = jnp.clip(jax.random.normal(subkey, (NDOF, NDOF), jnp.float32), -4.0, 4.0)
    return near_identity(noise, 0.5)


def draw_coarse_inv(key, part):
    first_key = jax.random.fold_in(key, 31)
    second_key = jax.random.fold_in(key, 32)
    bound_off = 2.0 / CW
    upper = jax.random.uniform(first_key, (NAGG, CW, CW), jnp.float32, -bound_off, bound_off)
    symmetric = 0.5 * (upper + jnp.transpose(upper, (0, 2, 1)))
    diagonal = jnp.exp(jax.random.uniform(second_key, (NAGG, CW), jnp.float32, math.log(2.5), math.log(5.0)))
    identity = jnp.eye(CW, dtype=jnp.float32)
    factor = 1.0 / math.sqrt(max(E_DEV // AGG_DEV, 1))
    return factor * (symmetric * (1.0 - identity)[None] + identity[None] * diagonal[:, :, None])


def grid_place(index_part):
    half_rest = NPART // 8
    coord_x = index_part % 4
    rest = index_part // 4
    folded = 2 * (rest % half_rest) + rest // half_rest
    return (coord_x, folded % 4, folded // 4)


def draw_peer_slots(key, part):
    weight_key = jax.random.fold_in(key, 41)
    count_key = jax.random.fold_in(key, 42)
    first_key = jax.random.fold_in(key, 43)
    second_key = jax.random.fold_in(key, 44)
    elem_key = jax.random.fold_in(key, 45)
    index_part = jnp.arange(NPART, dtype=jnp.int32)
    coord_x, coord_y, coord_z = grid_place(index_part)
    touching = (jnp.abs(coord_x[:, None] - coord_x[None, :]) <= 1) & (jnp.abs(coord_y[:, None] - coord_y[None, :]) <= 1) & (jnp.abs(coord_z[:, None] - coord_z[None, :]) <= 1)
    weights = jax.random.randint(weight_key, (NPART,), 1, 5)
    raw_counts = jax.random.randint(count_key, (NPART, NPART), CAP // 2, CAP + 1)
    rows = index_part[:, None]
    cols = index_part[None, :]
    paired = jnp.where(rows < cols, raw_counts, raw_counts.T)
    counts = jnp.minimum(CAP, jnp.maximum(1, paired * (weights[:, None] + weights[None, :]) // 5))
    counts = jnp.where(touching & (rows != cols), counts, 0)
    first_part = 4 * jax.random.randint(first_key, (), 0, NPART // 4) + jax.random.randint(second_key, (), 0, 3)
    second_part = first_part + 1
    full_pair = (rows == first_part) & (cols == second_part) | (rows == second_part) & (cols == first_part)
    counts = jnp.where(full_pair, CAP, counts)
    elements = jax.random.randint(elem_key, (NPART, NPART, CAP), 0, E_DEV)
    slot_index = jnp.arange(CAP)[None, None, :]
    return jnp.where(slot_index < counts[:, :, None], elements, -1).astype(jnp.int32)


def draw_local_pairs(key, part):
    first_key = jax.random.fold_in(key, 51)
    second_key = jax.random.fold_in(key, 52)
    first_end = jax.random.randint(first_key, (NLP,), 0, E_DEV)
    offset = jax.random.randint(second_key, (NLP,), 1, E_DEV)
    second_end = (first_end + offset) % E_DEV
    return jnp.stack([first_end, second_end]).astype(jnp.int32)


def touch_ends(values, rng, smallest, top_value):
    longest = values.shape.index(max(values.shape))
    spots = []
    for shift in (0, 1):
        where = [jax.random.randint(jax.random.fold_in(rng, axis), (), 0, length) for axis, length in enumerate(values.shape)]
        where[longest] = (where[longest] + shift) % values.shape[longest]
        spots.append(tuple(where))
    return values.at[spots[0]].set(smallest).at[spots[1]].set(top_value)


def block_scale(stream_key, extent, cuts, low, high):
    def one(dim, shards_of):
        steps = jax.random.uniform(jax.random.fold_in(jax.random.fold_in(stream_key, 6), dim), (shards_of,), jnp.float32, low / len(cuts), high / len(cuts))
        return jnp.repeat(jnp.exp(steps), extent[dim] // shards_of).reshape((-1,) + (1,) * (len(extent) - dim - 1))

    gain = one(*cuts[0])
    for cut in cuts[1:]:
        gain = gain * one(*cut)
    return gain


def normal_values(key, shape, deviation, bound, kind=jnp.bfloat16):
    return jnp.clip(deviation * jax.random.normal(key, shape, jnp.float32), -bound, bound).astype(kind)


def setup_inputs(seed: int = 0) -> dict:
    streams_of = jax.random.split(jax.random.key(seed), 13)
    return {
        "probes": draw_probes(jax.random.fold_in(streams_of[12], 71), 0),
        "viscosity": jnp.clip(jnp.exp(math.log(10.0) - 4.6051702 * jax.random.uniform(streams_of[1], (NDOF, NE), jnp.float32) ** block_scale(streams_of[1], (NDOF, NE), ((1, 64),), -0.2, 0.2)), 0.1, 10.0),
        "friction": jnp.clip(jnp.exp(math.log(1.0) - 2.9957323 * jax.random.uniform(streams_of[2], (NDOF, NE), jnp.float32) ** block_scale(streams_of[2], (NDOF, NE), ((1, 64),), -0.2, 0.2)), 0.05, 1.0),
        "sensitivity": jnp.clip(jnp.exp(math.log(3.0) - 1.7917595 * jax.random.uniform(streams_of[3], (NDOF, NE), jnp.float32) ** block_scale(streams_of[3], (NDOF, NE), ((1, 64),), -0.2, 0.2)), 0.5, 3.0),
        "misfit_weight": jnp.clip(jnp.exp(math.log(10.0) - 2.3025851 * jax.random.uniform(streams_of[4], (NDOF, NE), jnp.float32) ** block_scale(streams_of[4], (NDOF, NE), ((1, 64),), -0.2, 0.2)), 1.0, 10.0),
        "grad_ref": draw_grad_ref(jax.random.fold_in(streams_of[12], 71), 0),
        "trace_ref": draw_trace_ref(jax.random.fold_in(streams_of[12], 71), 0),
        "coarse_modes": normal_values(streams_of[7], (NDOF, CW), NDOF ** -0.5, 0.4375, jnp.float32),
        "coarse_inv": draw_coarse_inv(jax.random.fold_in(streams_of[12], 71), 0),
        "peer_slots": draw_peer_slots(jax.random.fold_in(streams_of[12], 71), 0),
        "local_pairs": draw_local_pairs(jax.random.fold_in(streams_of[12], 71), 0),
        "elem_agg": touch_ends(jax.random.randint(streams_of[11], (NE,), 0, GROUP_AGG), jax.random.fold_in(streams_of[11], 1), 0, GROUP_AGG - 1).astype(jnp.int32),
    }


highest = lax.Precision.HIGHEST
relax_weight = 0.6


def matmul(left, right):
    return jnp.dot(left, right, precision=highest, preferred_element_type=jnp.float32)


def reference(probes, viscosity, friction, sensitivity, misfit_weight, grad_ref, trace_ref, coarse_modes, coarse_inv, peer_slots, local_pairs, elem_agg):
    part_total = N_LEAF * N_AGG
    elem_total = E_DEV * part_total
    part_index = jnp.arange(part_total, dtype=jnp.int32)
    filled = peer_slots >= 0
    mirror = jnp.transpose(peer_slots, (1, 0, 2))
    own_global = jnp.where(filled, part_index[:, None, None] * E_DEV + peer_slots, 0).reshape(-1).astype(jnp.int32)
    other_global = jnp.where(filled, part_index[None, :, None] * E_DEV + mirror, 0).reshape(-1).astype(jnp.int32)
    filled_float = filled.reshape(-1).astype(jnp.float32)
    pair_base = ((jnp.arange(local_pairs.shape[1], dtype=jnp.int32) // E_DEV) * E_DEV).astype(jnp.int32)
    first_end = (local_pairs[0] + pair_base).astype(jnp.int32)
    second_end = (local_pairs[1] + pair_base).astype(jnp.int32)
    counts = jnp.zeros((elem_total,), jnp.float32)
    counts = counts.at[first_end].add(1.0).at[second_end].add(1.0).at[own_global].add(filled_float)
    trace_square = jnp.sum(trace_ref * trace_ref, axis=0)
    diag_op = matmul((grad_ref * grad_ref).T, viscosity) + friction + counts[None, :] * trace_square[:, None]
    agg_index = ((jnp.arange(elem_total, dtype=jnp.int32) // (E_DEV * N_AGG)) * GROUP_AGG + elem_agg).astype(jnp.int32)

    def operate(field_vec):
        inner_term = matmul(grad_ref.T, viscosity * matmul(grad_ref, field_vec))
        traces = matmul(trace_ref, field_vec)
        local_diff = traces[:, first_end] - traces[:, second_end]
        cross_diff = (traces[:, own_global] - traces[:, other_global]) * filled_float[None, :]
        accumulated = jnp.zeros_like(field_vec)
        accumulated = accumulated.at[:, first_end].add(local_diff).at[:, second_end].add(-local_diff)
        accumulated = accumulated.at[:, own_global].add(cross_diff)
        return inner_term + friction * field_vec + matmul(trace_ref.T, accumulated)

    def coarse(residual_now):
        projected = matmul(coarse_modes.T, residual_now)
        coarse_sums = jax.ops.segment_sum(projected.T, agg_index, num_segments=NAGG).T
        solved = jnp.einsum("acd,da->ca", coarse_inv, coarse_sums, precision=highest)
        return matmul(coarse_modes, solved[:, agg_index])

    def precond(residual_now):
        smooth = relax_weight * residual_now / diag_op
        for sweep_index in range(SWEEPS - 1):
            smooth = smooth + relax_weight * (residual_now - operate(smooth)) / diag_op
        return smooth + coarse(residual_now)

    def krylov(source):
        residual_now = source
        precon = precond(residual_now)
        search = precon
        energy_now = jnp.sum(residual_now * precon)
        iterate = jnp.zeros_like(source)
        for iteration in range(ITERS):
            image_vec = operate(search)
            step_size = energy_now / jnp.sum(search * image_vec)
            iterate = iterate + step_size * search
            if iteration + 1 < ITERS:
                residual_now = residual_now - step_size * image_vec
                precon = precond(residual_now)
                energy_next = jnp.sum(residual_now * precon)
                search = precon + (energy_next / energy_now) * search
                energy_now = energy_next
        return iterate

    velocities = []
    hessians = []
    for probe_index in range(PROBES):
        forward = krylov(sensitivity * probes[probe_index])
        adjoint = krylov(misfit_weight * forward)
        velocities.append(forward)
        hessians.append(sensitivity * adjoint)
    velocity_stack = jnp.stack(velocities)
    hessian_stack = jnp.stack(hessians)
    trace_value = jnp.sum(probes * hessian_stack) / PROBES
    return velocity_stack, hessian_stack, trace_value
```

```python
import functools
import jax
import jax.numpy as jnp
from jax import lax
from jax.experimental import pallas as pl
from jax.experimental.pallas import tpu as pltpu
from jax.sharding import PartitionSpec as P

MESH = pl.DeviceIdType.MESH
F32 = jnp.float32
BF16 = jnp.bfloat16
AXES = ("leaf", "agg", "probe")
RELAX = 0.6
CAP = 16
NT = (((1,), (1,)), ((), ()))
X = 4

RELOCATE = True


def split(value):
    high = value.astype(BF16)
    return high, (value - high.astype(F32)).astype(BF16)


def dot(left, right):
    return jnp.dot(left, right, preferred_element_type=F32)


def dot_exact(left, right_pair):
    return dot(left, right_pair[0]) + dot(left, right_pair[1])


def dot_split(left, right_pair):
    left_high, left_low = split(left)
    return dot(left_high, right_pair[0]) + (
        dot(left_low, right_pair[0]) + dot(left_high, right_pair[1])
    )


def place(unit, probe, probes):
    leaf, agg = unit // 2, unit % 2
    if not RELOCATE:
        return leaf, agg, probe
    z, x = leaf // X, leaf % X
    pair = leaf_pair(probes)
    return (probe * pair + z % pair) * X + x, agg, z // pair


def leaf_pair(probes):
    return 2


def kernel(
    parts,
    probes,
    fields,
    grad,
    trace,
    modes,
    inv,
    ints,
    out,
    trace_out,
    weights_h,
    weights_l,
    modes_h,
    modes_l,
    modes_t_h,
    modes_t_l,
    inv_h,
    inv_l,
    scatter,
    scatter_two,
    gather,
    gather_two,
    adjacent,
    group_sum,
    group_spread,
    visc,
    fric,
    misfit,
    inv_diag,
    count,
    probe_sens,
    rhs,
    first_dir,
    image,
    pre,
    traces,
    send,
    recv,
    sums,
    sums_in,
    solved,
    dots_a,
    dots_b,
    traces_all,
    send_sem,
    recv_sem,
    coarse_send_sem,
    coarse_recv_sem,
    dots_send_sem,
    dots_recv_sem,
    last_send_sem,
    last_recv_sem,
):
    leaf, agg, along = lax.axis_index("leaf"), lax.axis_index("agg"), lax.axis_index("probe")
    if RELOCATE:
        z, x = leaf // X, leaf % X
        probe = z // 2
        unit = ((along * 2 + z % 2) * X + x) * 2 + agg
    else:
        probe = along
        unit = leaf * 2 + agg
    sibling = (leaf, 1 - agg, along)
    ndof = grad.shape[0]
    elems = fields.shape[2]
    halves = CAP // 2
    others = parts - 1

    def partner(step):
        return lax.rem(unit + step, parts)

    barrier = pltpu.get_barrier_semaphore()

    @pl.loop(1, parts)
    def _(step):
        pl.semaphore_signal(
            barrier, inc=1, device_id=place(partner(step), probe, probes), device_id_type=MESH
        )

    @pl.loop(1, probes)
    def _(step):
        pl.semaphore_signal(
            barrier,
            inc=1,
            device_id=place(unit, lax.rem(probe + step, probes), probes),
            device_id_type=MESH,
        )

    for slot, matrix in enumerate((grad[...].T, grad[...], trace[...].T, trace[...])):
        weights_h[slot], weights_l[slot] = split(matrix)
    modes_h[...], modes_l[...] = split(modes[...])
    modes_t_h[...], modes_t_l[...] = split(modes[...].T)
    for block in range(inv.shape[0]):
        inv_h[block], inv_l[block] = split(inv[block])
    rows = lax.broadcasted_iota(jnp.int32, (elems, elems), 0).astype(F32)

    def one_hot(row):
        return (ints[pl.ds(row, 1), :] == rows).astype(F32)

    slots = parts * CAP
    cross = jnp.zeros((elems, 1), F32)
    for block in range(slots // elems):
        hot = one_hot(block)
        cross = cross + jnp.sum(hot, axis=1, keepdims=True)
        here = pl.ds(block * elems, elems)
        scatter[:, here] = hot.astype(BF16)
        hot_t = hot.T
        gather[here, :] = hot_t.astype(BF16)
        paired = hot_t.reshape(elems // CAP, 2, halves, elems)
        low = paired[:, 0].reshape(elems // 2, elems)
        high = paired[:, 1].reshape(elems // 2, elems)
        half = pl.ds(block * (elems // 2), elems // 2)
        gather_two[half, :elems] = low.astype(BF16)
        gather_two[half, elems:] = high.astype(BF16)
    for block in range(slots // elems // 2):
        here = pl.ds(block * elems, elems)
        scatter_two[:elems, here] = gather_two[here, :elems].astype(F32).T.astype(BF16)
        scatter_two[elems:, here] = gather_two[here, elems:].astype(F32).T.astype(BF16)
    base = slots // elems
    ends = [one_hot(base + end).astype(BF16) for end in range(2)]
    near = lax.dot_general(ends[0], ends[1], NT, preferred_element_type=F32)
    near = near + lax.dot_general(ends[1], ends[0], NT, preferred_element_type=F32)
    adjacent[...] = near.astype(BF16)
    count[...] = cross + jnp.sum(near, axis=1, keepdims=True)
    hot = one_hot(base + 2)
    group_sum[...] = hot[: sums.shape[0]].astype(BF16)
    group_spread[...] = hot.T.astype(BF16)

    visc[...] = fields[1].T
    fric[...] = fields[2].T
    misfit[...] = fields[4].T
    square = grad[...] * grad[...]
    trace_square = jnp.sum(trace[...] * trace[...], axis=0, keepdims=True)
    diag = dot_split(visc[...], split(square)) + fric[...] + count[...] * trace_square
    inv_diag[...] = RELAX / diag
    start = (fields[3] * fields[0]).T
    probe_sens[...] = start
    rhs[...] = start
    solved[...] = jnp.zeros_like(solved)
    for turn in range(2):
        recv[turn, unit] = jnp.zeros(recv.shape[2:], F32)
    pl.semaphore_wait(barrier, others + probes - 1)

    def weight(slot):
        return weights_h[slot], weights_l[slot]

    def block_copy(turn, peer):
        return pltpu.make_async_remote_copy(
            src_ref=send.at[turn, peer],
            dst_ref=recv.at[turn, unit],
            send_sem=send_sem.at[turn],
            recv_sem=recv_sem.at[turn],
            device_id=place(peer, probe, probes),
            device_id_type=MESH,
        )

    def wait_blocks(turn, sem):
        blocks = recv.at[turn, pl.ds(0, others)]
        pltpu.make_async_copy(blocks, blocks, sem.at[turn]).wait()

    def operate(value, turn):
        traced = dot_split(value, weight(2))
        high, low = split(traced)
        blank = jnp.zeros((elems, 2 * elems - ndof), BF16)
        send[turn, :, :CAP, :] = dot_exact(
            gather[...], (high[:, :elems], low[:, :elems])
        ).reshape(parts, CAP, elems)

        def two(piece):
            rest = piece[:, elems:]
            return jnp.concatenate(
                [jnp.concatenate([rest, blank], 1), jnp.concatenate([blank, rest], 1)], 0
            )

        send[turn, :, CAP:, :] = dot_exact(gather_two[...], (two(high), two(low))).reshape(
            parts, halves, elems
        )

        @pl.loop(1, parts)
        def _(step):
            block_copy(turn, partner(step)).start()

        inner = dot_split(visc[...] * dot_split(value, weight(0)), weight(1))
        near = count[...] * traced - dot_exact(adjacent[...], (high, low))
        inner = inner + fric[...] * value
        wait_blocks(turn, recv_sem)
        first = dot_exact(scatter[...], split(recv[turn, :, :CAP, :].reshape(slots, elems)))
        second = dot_exact(
            scatter_two[...], split(recv[turn, :, CAP:, :].reshape(slots // 2, elems))
        )
        rest = 2 * elems - ndof
        second = second[:elems, :rest] + second[elems:, rest:]
        near = near - jnp.concatenate([first, second], 1)
        result = inner + dot_split(near, weight(3))
        wait_blocks(turn, send_sem)
        return result

    own_rows = pl.ds(pl.multiple_of(agg * 8, 8), 8)
    peer_rows = pl.ds(pl.multiple_of((1 - agg) * 8, 8), 8)
    sums_copy = pltpu.make_async_remote_copy(
        src_ref=sums.at[peer_rows],
        dst_ref=sums_in,
        send_sem=coarse_send_sem.at[0],
        recv_sem=coarse_recv_sem.at[0],
        device_id=sibling,
        device_id_type=MESH,
    )
    solved_copy = pltpu.make_async_remote_copy(
        src_ref=solved.at[own_rows],
        dst_ref=solved.at[own_rows],
        send_sem=coarse_send_sem.at[1],
        recv_sem=coarse_recv_sem.at[1],
        device_id=sibling,
        device_id_type=MESH,
    )

    def coarse_start(residual):
        projected = dot_split(residual, (modes_h[...], modes_l[...]))
        sums[...] = dot_exact(group_sum[...], split(projected))
        sums_copy.start()

    def coarse_solve():
        sums_copy.wait()
        total = sums[own_rows, :] + sums_in[...]
        row = lax.broadcasted_iota(jnp.int32, total.shape, 0)
        result = jnp.zeros_like(total)
        for block in range(total.shape[0]):
            one = dot_split(total, (inv_h[block], inv_l[block]))
            result = jnp.where(row == block, one, result)
        solved[own_rows, :] = result
        solved_copy.start()

    def coarse_end():
        solved_copy.wait()
        spread = dot_exact(group_spread[...], split(solved[...]))
        return dot_split(spread, (modes_t_h[...], modes_t_l[...]))

    def precondition(residual_ref, turn):
        residual = residual_ref[...]
        coarse_start(residual)
        pre[...] = residual * inv_diag[...]
        pre[...] += (residual_ref[...] - operate(pre[...], turn)) * inv_diag[...]
        coarse_solve()
        pre[...] += (residual_ref[...] - operate(pre[...], 1 - turn)) * inv_diag[...]
        return pre[...] + coarse_end()

    def lanes(left, right):
        total = jnp.sum(left * right, axis=0, keepdims=True)
        tail = jnp.concatenate(
            [total[:, elems:], jnp.zeros((1, 2 * elems - ndof), F32)], 1
        )
        return total[:, :elems] + tail

    def dots_copy(buffer, which, peer):
        return pltpu.make_async_remote_copy(
            src_ref=buffer.at[unit],
            dst_ref=buffer.at[unit],
            send_sem=dots_send_sem.at[which],
            recv_sem=dots_recv_sem.at[which],
            device_id=place(peer, probe, probes),
            device_id_type=MESH,
        )

    def dots_start(buffer, which, pieces):
        pad = 8 - len(pieces)
        buffer[unit] = jnp.concatenate(list(pieces) + [jnp.zeros((pad, elems), F32)], 0)

        @pl.loop(1, parts)
        def _(step):
            dots_copy(buffer, which, partner(step)).start()

    def dots_end(buffer, which):
        blocks = buffer.at[pl.ds(0, others)]
        pltpu.make_async_copy(blocks, blocks, dots_recv_sem.at[which]).wait()
        pltpu.make_async_copy(blocks, blocks, dots_send_sem.at[which]).wait()
        total = jnp.sum(jnp.sum(buffer[...], axis=0), axis=1, keepdims=True)
        return [total[row : row + 1] for row in range(8)]

    @pl.loop(0, 2)
    def _(solve):
        first_dir[...] = precondition(rhs, 0)
        image[...] = operate(first_dir[...], 0)
        dots_start(
            dots_a,
            0,
            [lanes(rhs[...], first_dir[...]), lanes(first_dir[...], image[...])],
        )
        second = precondition(image, 1)
        energy, curve, *_ = dots_end(dots_a, 0)
        step = energy / curve
        second = first_dir[...] - step * second
        residual = rhs[...] - step * image[...]
        pre[...] = second
        second_image = operate(pre[...], 1)
        second = pre[...]
        dots_start(
            dots_b,
            1,
            [
                lanes(residual, second),
                lanes(second, second_image),
                lanes(second, image[...]),
                lanes(probe_sens[...], first_dir[...]),
                lanes(probe_sens[...], second),
            ],
        )
        energy_next, curve_zz, curve_zp, trace_first, trace_second, *_ = dots_end(dots_b, 1)
        ratio = energy_next / energy
        curve_next = curve_zz + 2.0 * ratio * curve_zp + ratio * ratio * curve
        step_next = energy_next / curve_next
        weight_first = step + step_next * ratio
        result = weight_first * first_dir[...] + step_next * pre[...]
        rhs[...] = misfit[...] * result
        out[solve] = result.T
        value = weight_first * trace_first + step_next * trace_second
        traces[...] = jnp.broadcast_to(value, traces.shape)

    out[1] = out[1] * fields[3]
    traces_all[probe] = traces[...]

    def last_copy(step):
        return pltpu.make_async_remote_copy(
            src_ref=traces,
            dst_ref=traces_all.at[probe],
            send_sem=last_send_sem,
            recv_sem=last_recv_sem,
            device_id=place(unit, lax.rem(probe + step, probes), probes),
            device_id_type=MESH,
        )

    @pl.loop(1, probes)
    def _(step):
        last_copy(step).start()

    blocks = traces_all.at[pl.ds(0, probes - 1)]
    pltpu.make_async_copy(blocks, blocks, last_recv_sem).wait()
    pltpu.make_async_copy(blocks, blocks, last_send_sem).wait()
    trace_out[...] = jnp.sum(traces_all[...], axis=0) / probes


def on_device(
    probes,
    viscosity,
    friction,
    sensitivity,
    misfit_weight,
    grad_ref,
    trace_ref,
    coarse_modes,
    coarse_inv,
    peer_slots,
    local_pairs,
    elem_agg,
):
    leaves, aggs, count = (lax.axis_size(axis) for axis in AXES)
    parts = leaves * aggs
    ndof, elems = viscosity.shape
    own_aggs, modes_n = coarse_inv.shape[:2]
    slots = parts * CAP
    ints = jnp.concatenate(
        [
            peer_slots.reshape(slots // elems, elems),
            local_pairs,
            elem_agg[None],
            jnp.zeros((5, elems), jnp.int32),
        ]
    ).astype(F32)
    fields = jnp.stack([probes[0], viscosity, friction, sensitivity, misfit_weight])
    if RELOCATE:
        moves = []
        for unit in range(parts):
            for probe in range(count):
                leaf, agg, along = place(unit, probe, count)
                moves.append((unit * count + probe, (leaf * aggs + agg) * count + along))
        back = [(to, source) for source, to in moves]
        fields = lax.ppermute(fields, AXES, moves)
        ints = lax.ppermute(ints, AXES, moves)
        coarse_inv = lax.ppermute(coarse_inv, AXES, moves)

    def vmem(*shape, dtype=F32):
        return pltpu.VMEM(shape, dtype)

    field = vmem(elems, ndof)
    scratch = [
        vmem(4, ndof, ndof, dtype=BF16),
        vmem(4, ndof, ndof, dtype=BF16),
        vmem(ndof, modes_n, dtype=BF16),
        vmem(ndof, modes_n, dtype=BF16),
        vmem(modes_n, ndof, dtype=BF16),
        vmem(modes_n, ndof, dtype=BF16),
        vmem(own_aggs, modes_n, modes_n, dtype=BF16),
        vmem(own_aggs, modes_n, modes_n, dtype=BF16),
        vmem(elems, slots, dtype=BF16),
        vmem(2 * elems, slots // 2, dtype=BF16),
        vmem(slots, elems, dtype=BF16),
        vmem(slots // 2, 2 * elems, dtype=BF16),
        vmem(elems, elems, dtype=BF16),
        vmem(aggs * own_aggs, elems, dtype=BF16),
        vmem(elems, elems, dtype=BF16),
        field,
        field,
        field,
        field,
        vmem(elems, 1),
        field,
        field,
        field,
        field,
        field,
        vmem(8, elems),
        vmem(2, parts, CAP + CAP // 2, elems),
        vmem(2, parts, CAP + CAP // 2, elems),
        vmem(aggs * own_aggs, modes_n),
        vmem(own_aggs, modes_n),
        vmem(elems, modes_n),
        vmem(parts, 8, elems),
        vmem(parts, 8, elems),
        vmem(count, 8, elems),
        pltpu.SemaphoreType.DMA((2,)),
        pltpu.SemaphoreType.DMA((2,)),
        pltpu.SemaphoreType.DMA((2,)),
        pltpu.SemaphoreType.DMA((2,)),
        pltpu.SemaphoreType.DMA((2,)),
        pltpu.SemaphoreType.DMA((2,)),
        pltpu.SemaphoreType.DMA,
        pltpu.SemaphoreType.DMA,
    ]
    out, trace_tile = pl.pallas_call(
        functools.partial(kernel, parts, count),
        out_shape=(
            jax.ShapeDtypeStruct((2, ndof, elems), F32),
            jax.ShapeDtypeStruct((8, elems), F32),
        ),
        in_specs=[pl.BlockSpec(memory_space=pltpu.VMEM)] * 6,
        out_specs=(pl.BlockSpec(memory_space=pltpu.VMEM),) * 2,
        scratch_shapes=scratch,
        compiler_params=pltpu.CompilerParams(
            collective_id=0, has_side_effects=True, vmem_limit_bytes=48 * 1024 * 1024
        ),
    )(fields, grad_ref, trace_ref, coarse_modes, coarse_inv, ints)
    if RELOCATE:
        out = lax.ppermute(out, AXES, back)
    return out[0][None], out[1][None], trace_tile[0, 0]


def solution(mesh):
    in_specs = (
        P("probe", None, ("leaf", "agg")),
        P(None, ("leaf", "agg")),
        P(None, ("leaf", "agg")),
        P(None, ("leaf", "agg")),
        P(None, ("leaf", "agg")),
        P(),
        P(),
        P(),
        P(("leaf", "agg"), None, None),
        P(("leaf", "agg"), None, None),
        P(None, ("leaf", "agg")),
        P(("leaf", "agg")),
    )
    out_specs = (P("probe", None, ("leaf", "agg")), P("probe", None, ("leaf", "agg")), P())
    return jax.shard_map(
        on_device, mesh=mesh, in_specs=in_specs, out_specs=out_specs, check_vma=False
    )
```

```python
import functools
import jax
import jax.numpy as jnp
from jax import lax
from jax.experimental import pallas as pl
from jax.experimental.pallas import tpu as pltpu
from jax.sharding import PartitionSpec as P

MESH = pl.DeviceIdType.MESH
F32 = jnp.float32
BF16 = jnp.bfloat16
AXES = ("leaf", "agg", "probe")
RELAX = 0.6
CAP = 16
NT = (((1,), (1,)), ((), ()))
X = 4

PAIR = 2


def split(value):
    high = value.astype(BF16)
    return high, (value - high.astype(F32)).astype(BF16)


def dot(left, right):
    return jnp.dot(left, right, preferred_element_type=F32)


def dot_exact(left, right_pair):
    return dot(left, right_pair[0]) + dot(left, right_pair[1])


def dot_split(left, right_pair):
    left_high, left_low = split(left)
    return dot(left_high, right_pair[0]) + (
        dot(left_low, right_pair[0]) + dot(left_high, right_pair[1])
    )


def group_steps(probes):
    def hops(step):
        return -(min(step[0], probes - step[0]) + step[1] + min(step[2], X - step[2]))

    steps = [
        (y, z, x, core)
        for y in range(probes)
        for z in range(PAIR)
        for x in range(X)
        for core in range(2)
    ][1:]
    return sorted(steps, key=hops)


def kernel(
    parts,
    probes,
    probe_in,
    visc_in,
    fric_in,
    sens_in,
    misfit_in,
    grad,
    trace,
    modes,
    inv,
    ints_in,
    out,
    trace_out,
    weights_h,
    weights_l,
    modes_h,
    modes_l,
    modes_t_h,
    modes_t_l,
    inv_h,
    inv_l,
    scatter,
    scatter_two,
    gather,
    gather_two,
    adjacent,
    group_sum,
    group_spread,
    visc,
    fric,
    misfit,
    inv_diag,
    count,
    probe_sens,
    rhs,
    first_dir,
    image,
    pre,
    traces,
    home,
    moved,
    ints,
    result_out,
    result_in,
    send,
    recv,
    sums,
    sums_in,
    solved_own,
    solved,
    dots_a,
    dots_b,
    traces_all,
    send_sem,
    recv_sem,
    move_send_sem,
    move_recv_sem,
    coarse_send_sem,
    coarse_recv_sem,
    dots_send_sem,
    dots_recv_sem,
    last_send_sem,
    last_recv_sem,
):
    leaf, core, along = lax.axis_index("leaf"), lax.axis_index("agg"), lax.axis_index("probe")
    z, x = lax.div(leaf, X), lax.rem(leaf, X)
    probe, low = lax.div(z, PAIR), lax.rem(z, PAIR)
    unit = ((along * PAIR + low) * X + x) * 2 + core
    mirror_leaf = (along * PAIR + low) * X + x
    at_home = along == probe
    ndof = grad.shape[0]
    elems = visc_in.shape[1]
    slots = parts * CAP
    halves = CAP // 2
    others = parts - 1
    rest = 2 * elems - ndof

    lows = [lax.rem(low + step, PAIR) for step in range(PAIR)]
    xs = [lax.rem(x + step, X) for step in range(X)]
    cores = [core, 1 - core]
    alongs = [lax.rem(along + step, probes) for step in range(probes)]
    leaves = [[(probe * PAIR + part) * X + place for place in xs] for part in lows]
    peers = []
    for y_step, z_step, x_step, core_step in group_steps(probes):
        device = (leaves[z_step][x_step], cores[core_step], alongs[y_step])
        peer = ((alongs[y_step] * PAIR + lows[z_step]) * X + xs[x_step]) * 2 + cores[core_step]
        peers.append((device, peer))
    mates = [
        ((lax.rem(probe + step, probes) * PAIR + low) * X + x, core, along)
        for step in range(1, probes)
    ]
    mirrors = [(mirror_leaf, side, probe) for side in cores]

    barrier = pltpu.get_barrier_semaphore()
    for device in [device for device, _ in peers] + mates:
        pl.semaphore_signal(barrier, inc=1, device_id=device, device_id_type=MESH)

    @pl.when(jnp.logical_not(at_home))
    def _():
        for device in mirrors:
            pl.semaphore_signal(barrier, inc=1, device_id=device, device_id_type=MESH)

    def wait_bytes(ref, sem):
        pltpu.make_async_copy(ref, ref, sem).wait()

    def mirror_start(source, target, send_at, recv_at, step=0):
        def remote():
            return pltpu.make_async_remote_copy(
                src_ref=source,
                dst_ref=target,
                send_sem=send_at,
                recv_sem=recv_at,
                device_id=mirrors[step],
                device_id_type=MESH,
            )

        if step:
            remote().start()
        else:

            @pl.when(at_home)
            def _():
                pltpu.make_async_copy(source, target, recv_at).start()

            @pl.when(jnp.logical_not(at_home))
            def _():
                remote().start()

    def mirror_sent(source, send_at, step=0):
        if step:
            wait_bytes(source, send_at)
        else:

            @pl.when(jnp.logical_not(at_home))
            def _():
                wait_bytes(source, send_at)

    rows = lax.broadcasted_iota(jnp.int32, (elems, elems), 0).astype(F32)

    def one_hot(ref, row):
        return (ref[pl.ds(row, 1), :] == rows).astype(F32)

    base = slots // elems

    def adjacency(ref):
        ends = [one_hot(ref, base + end).astype(BF16) for end in range(2)]
        near = lax.dot_general(ends[0], ends[1], NT, preferred_element_type=F32)
        return near + lax.dot_general(ends[1], ends[0], NT, preferred_element_type=F32)

    home[0] = sens_in[...] * probe_in[0]
    touching = jnp.sum(adjacency(ints_in), axis=0, keepdims=True)
    for block in range(base):
        touching = touching + jnp.sum(one_hot(ints_in, block).T, axis=0, keepdims=True)
    grad_t, trace_t = grad[...].T, trace[...].T
    trace_square = jnp.sum(trace_t * trace_t, axis=1, keepdims=True)
    diag = dot_split(grad_t * grad_t, split(visc_in[...])) + fric_in[...]
    home[1] = RELAX / (diag + trace_square * touching)
    for turn in range(2):
        recv[turn, unit] = jnp.zeros(recv.shape[2:], F32)

    @pl.when(at_home)
    def _():
        pl.semaphore_wait(barrier, others + probes - 1)

    @pl.when(jnp.logical_not(at_home))
    def _():
        pl.semaphore_wait(barrier, others + probes + 1)

    sources = [ints_in, home.at[0], home.at[1], visc_in, fric_in, misfit_in]
    targets = [ints] + [moved.at[which] for which in range(5)]
    for which, (source, target) in enumerate(zip(sources, targets)):
        mirror_start(source, target, move_send_sem.at[which], move_recv_sem.at[which])

    def moved_end(which):
        wait_bytes(targets[which], move_recv_sem.at[which])
        mirror_sent(sources[which], move_send_sem.at[which])

    for slot, matrix in enumerate((grad_t, grad[...], trace_t, trace[...])):
        weights_h[slot], weights_l[slot] = split(matrix)
    modes_h[...], modes_l[...] = split(modes[...])
    modes_t_h[...], modes_t_l[...] = split(modes[...].T)
    for block in range(inv.shape[0]):
        inv_h[block], inv_l[block] = split(inv[block])
    moved_end(0)
    cross = jnp.zeros((elems, 1), F32)
    for block in range(base):
        hot = one_hot(ints, block)
        cross = cross + jnp.sum(hot, axis=1, keepdims=True)
        here = pl.ds(block * elems, elems)
        scatter[:, here] = hot.astype(BF16)
        hot_t = hot.T
        gather[here, :] = hot_t.astype(BF16)
        paired = hot_t.reshape(elems // CAP, 2, halves, elems)
        half = pl.ds(block * (elems // 2), elems // 2)
        gather_two[half, :elems] = paired[:, 0].reshape(elems // 2, elems).astype(BF16)
        gather_two[half, elems:] = paired[:, 1].reshape(elems // 2, elems).astype(BF16)
    for block in range(base // 2):
        here = pl.ds(block * elems, elems)
        scatter_two[:elems, here] = gather_two[here, :elems].astype(F32).T.astype(BF16)
        scatter_two[elems:, here] = gather_two[here, elems:].astype(F32).T.astype(BF16)
    near_pairs = adjacency(ints)
    adjacent[...] = near_pairs.astype(BF16)
    count[...] = cross + jnp.sum(near_pairs, axis=1, keepdims=True)
    hot = one_hot(ints, base + 2)
    group_sum[...] = hot[: sums.shape[0]].astype(BF16)
    group_spread[...] = hot.T.astype(BF16)
    moved_end(1)
    start = moved[0].T
    probe_sens[...] = start
    rhs[...] = start
    solved[...] = jnp.zeros_like(solved)
    moved_end(2)
    inv_diag[...] = moved[1].T

    def weight(slot):
        return weights_h[slot], weights_l[slot]

    def wait_blocks(turn, sem):
        wait_bytes(recv.at[turn, pl.ds(0, others)], sem.at[turn])

    def operate(value, turn, started=None):
        traced = dot_split(value, weight(2))
        high, low_part = split(traced)
        blank = jnp.zeros((elems, rest), BF16)
        send[turn, :, :CAP, :] = dot_exact(
            gather[...], (high[:, :elems], low_part[:, :elems])
        ).reshape(parts, CAP, elems)

        def two(piece):
            tail = piece[:, elems:]
            return jnp.concatenate(
                [jnp.concatenate([tail, blank], 1), jnp.concatenate([blank, tail], 1)], 0
            )

        send[turn, :, CAP:, :] = dot_exact(
            gather_two[...], (two(high), two(low_part))
        ).reshape(parts, halves, elems)
        for device, peer in peers:
            pltpu.make_async_remote_copy(
                src_ref=send.at[turn, peer],
                dst_ref=recv.at[turn, unit],
                send_sem=send_sem.at[turn],
                recv_sem=recv_sem.at[turn],
                device_id=device,
                device_id_type=MESH,
            ).start()
        if started is not None:
            started()
        inner = dot_split(visc[...] * dot_split(value, weight(0)), weight(1))
        near = count[...] * traced - dot_exact(adjacent[...], (high, low_part))
        inner = inner + fric[...] * value
        wait_blocks(turn, recv_sem)
        first = dot_exact(scatter[...], split(recv[turn, :, :CAP, :].reshape(slots, elems)))
        second = dot_exact(
            scatter_two[...], split(recv[turn, :, CAP:, :].reshape(slots // 2, elems))
        )
        second = second[:elems, :rest] + second[elems:, rest:]
        near = near - jnp.concatenate([first, second], 1)
        result = inner + dot_split(near, weight(3))
        wait_blocks(turn, send_sem)
        return result

    own_aggs = inv.shape[0]

    def agg_rows(side):
        return pl.ds(pl.multiple_of(side * own_aggs, own_aggs), own_aggs)

    def coarse_start(residual):
        projected = dot_split(residual, (modes_h[...], modes_l[...]))
        sums[...] = dot_exact(group_sum[...], split(projected))
        for step, side in enumerate(cores):
            mirror_start(
                sums.at[agg_rows(side)],
                sums_in.at[step],
                coarse_send_sem.at[step],
                coarse_recv_sem.at[step],
                step,
            )

    def coarse_solve():
        for step, side in enumerate(cores):
            wait_bytes(sums_in.at[step], coarse_recv_sem.at[step])
            mirror_sent(sums.at[agg_rows(side)], coarse_send_sem.at[step], step)
        total = sums_in[0] + sums_in[1]
        row = lax.broadcasted_iota(jnp.int32, total.shape, 0)
        result = jnp.zeros_like(total)
        for block in range(own_aggs):
            one = dot_split(total, (inv_h[block], inv_l[block]))
            result = jnp.where(row == block, one, result)
        solved_own[...] = result
        for step in range(2):
            mirror_start(
                solved_own,
                solved.at[agg_rows(core)],
                coarse_send_sem.at[2 + step],
                coarse_recv_sem.at[2 + step],
                step,
            )

    def coarse_end():
        for step, side in enumerate(cores):
            wait_bytes(solved.at[agg_rows(side)], coarse_recv_sem.at[2 + step])
            mirror_sent(solved_own, coarse_send_sem.at[2 + step], step)
        spread = dot_exact(group_spread[...], split(solved[...]))
        return dot_split(spread, (modes_t_h[...], modes_t_l[...]))

    def precondition(residual_ref, turn, started=None):
        pre[...] = residual_ref[...] * inv_diag[...]
        coarse_start(residual_ref[...])
        pre[...] += (residual_ref[...] - operate(pre[...], turn, started)) * inv_diag[...]
        coarse_solve()
        pre[...] += (residual_ref[...] - operate(pre[...], 1 - turn)) * inv_diag[...]
        return pre[...] + coarse_end()

    def lanes(left, right):
        total = jnp.sum(left * right, axis=0, keepdims=True)
        tail = jnp.concatenate([total[:, elems:], jnp.zeros((1, rest), F32)], 1)
        return total[:, :elems] + tail

    def dots_start(buffer, which, pieces):
        column = jnp.concatenate(list(pieces) + [jnp.zeros((8 - len(pieces), elems), F32)], 0)
        column = jnp.sum(column, axis=1, keepdims=True)
        across = lax.broadcasted_iota(jnp.int32, (8, elems), 1)
        down = lax.broadcasted_iota(jnp.int32, (8, elems), 0)
        buffer[unit] = jnp.sum(jnp.where(across == down, column, 0.0), axis=0, keepdims=True)
        for device, _ in peers:
            pltpu.make_async_remote_copy(
                src_ref=buffer.at[unit],
                dst_ref=buffer.at[unit],
                send_sem=dots_send_sem.at[which],
                recv_sem=dots_recv_sem.at[which],
                device_id=device,
                device_id_type=MESH,
            ).start()

    def dots_end(buffer, which):
        blocks = buffer.at[pl.ds(0, others)]
        wait_bytes(blocks, dots_recv_sem.at[which])
        wait_bytes(blocks, dots_send_sem.at[which])
        total = jnp.sum(buffer[...], axis=0)
        return [total[:, lane : lane + 1] for lane in range(8)]

    @pl.loop(0, 2)
    def _(solve):
        def first_time():
            @pl.when(solve == 0)
            def _():
                moved_end(3)
                visc[...] = moved[2].T
                moved_end(4)
                fric[...] = moved[3].T

        first_dir[...] = precondition(rhs, 0, first_time)
        image[...] = operate(first_dir[...], 0)
        dots_start(
            dots_a,
            0,
            [lanes(rhs[...], first_dir[...]), lanes(first_dir[...], image[...])],
        )
        second = precondition(image, 1)
        energy, curve, *_ = dots_end(dots_a, 0)
        step = energy / curve
        second = first_dir[...] - step * second
        residual = rhs[...] - step * image[...]
        pre[...] = second
        second_image = operate(pre[...], 1)
        second = pre[...]
        dots_start(
            dots_b,
            1,
            [
                lanes(residual, second),
                lanes(second, second_image),
                lanes(second, image[...]),
                lanes(probe_sens[...], first_dir[...]),
                lanes(probe_sens[...], second),
            ],
        )

        @pl.when(solve == 0)
        def _():
            moved_end(5)
            misfit[...] = moved[4].T

        energy_next, curve_zz, curve_zp, trace_first, trace_second, *_ = dots_end(dots_b, 1)
        ratio = energy_next / energy
        curve_next = curve_zz + 2.0 * ratio * curve_zp + ratio * ratio * curve
        step_next = energy_next / curve_next
        weight_first = step + step_next * ratio
        result = weight_first * first_dir[...] + step_next * pre[...]
        result_out[solve] = result.T
        mirror_start(
            result_out.at[solve],
            result_in.at[solve],
            move_send_sem.at[6 + solve],
            move_recv_sem.at[6 + solve],
        )
        rhs[...] = misfit[...] * result
        value = weight_first * trace_first + step_next * trace_second
        traces[...] = jnp.broadcast_to(value, traces.shape)

    traces_all[probe] = traces[...]
    for device in mates:
        pltpu.make_async_remote_copy(
            src_ref=traces,
            dst_ref=traces_all.at[probe],
            send_sem=last_send_sem,
            recv_sem=last_recv_sem,
            device_id=device,
            device_id_type=MESH,
        ).start()
    for solve in range(2):
        wait_bytes(result_in.at[solve], move_recv_sem.at[6 + solve])
        mirror_sent(result_out.at[solve], move_send_sem.at[6 + solve])
    out[0] = result_in[0]
    out[1] = result_in[1] * sens_in[...]
    blocks = traces_all.at[pl.ds(0, probes - 1)]
    wait_bytes(blocks, last_recv_sem)
    wait_bytes(blocks, last_send_sem)
    trace_out[...] = jnp.sum(traces_all[...], axis=0) / probes


def on_device(
    probes,
    viscosity,
    friction,
    sensitivity,
    misfit_weight,
    grad_ref,
    trace_ref,
    coarse_modes,
    coarse_inv,
    peer_slots,
    local_pairs,
    elem_agg,
):
    leaves, aggs, count = (lax.axis_size(axis) for axis in AXES)
    parts = leaves * aggs
    ndof, elems = viscosity.shape
    own_aggs, modes_n = coarse_inv.shape[:2]
    slots = parts * CAP
    ints = jnp.concatenate(
        [
            peer_slots.reshape(slots // elems, elems),
            local_pairs,
            elem_agg[None],
            jnp.zeros((5, elems), jnp.int32),
        ]
    ).astype(F32)

    def vmem(*shape, dtype=F32):
        return pltpu.VMEM(shape, dtype)

    field = vmem(elems, ndof)
    block_rows = CAP + CAP // 2
    dma = pltpu.SemaphoreType.DMA
    scratch = [
        vmem(4, ndof, ndof, dtype=BF16),
        vmem(4, ndof, ndof, dtype=BF16),
        vmem(ndof, modes_n, dtype=BF16),
        vmem(ndof, modes_n, dtype=BF16),
        vmem(modes_n, ndof, dtype=BF16),
        vmem(modes_n, ndof, dtype=BF16),
        vmem(own_aggs, modes_n, modes_n, dtype=BF16),
        vmem(own_aggs, modes_n, modes_n, dtype=BF16),
        vmem(elems, slots, dtype=BF16),
        vmem(2 * elems, slots // 2, dtype=BF16),
        vmem(slots, elems, dtype=BF16),
        vmem(slots // 2, 2 * elems, dtype=BF16),
        vmem(elems, elems, dtype=BF16),
        vmem(aggs * own_aggs, elems, dtype=BF16),
        vmem(elems, elems, dtype=BF16),
        field,
        field,
        field,
        field,
        vmem(elems, 1),
        field,
        field,
        field,
        field,
        field,
        vmem(8, elems),
        vmem(2, ndof, elems),
        vmem(5, ndof, elems),
        vmem(*ints.shape),
        vmem(2, ndof, elems),
        vmem(2, ndof, elems),
        vmem(2, parts, block_rows, elems),
        vmem(2, parts, block_rows, elems),
        vmem(aggs * own_aggs, modes_n),
        vmem(2, own_aggs, modes_n),
        vmem(own_aggs, modes_n),
        vmem(elems, modes_n),
        vmem(parts, 1, elems),
        vmem(parts, 1, elems),
        vmem(count, 8, elems),
        dma((2,)),
        dma((2,)),
        dma((8,)),
        dma((8,)),
        dma((4,)),
        dma((4,)),
        dma((2,)),
        dma((2,)),
        dma,
        dma,
    ]
    out, trace_tile = pl.pallas_call(
        functools.partial(kernel, parts, count),
        out_shape=(
            jax.ShapeDtypeStruct((2, ndof, elems), F32),
            jax.ShapeDtypeStruct((8, elems), F32),
        ),
        in_specs=[pl.BlockSpec(memory_space=pltpu.VMEM)] * 10,
        out_specs=(pl.BlockSpec(memory_space=pltpu.VMEM),) * 2,
        scratch_shapes=scratch,
        compiler_params=pltpu.CompilerParams(
            collective_id=0, has_side_effects=True, vmem_limit_bytes=48 * 1024 * 1024
        ),
    )(
        probes,
        viscosity,
        friction,
        sensitivity,
        misfit_weight,
        grad_ref,
        trace_ref,
        coarse_modes,
        coarse_inv,
        ints,
    )
    return out[0][None], out[1][None], trace_tile[0, 0]


def solution(mesh):
    in_specs = (
        P("probe", None, ("leaf", "agg")),
        P(None, ("leaf", "agg")),
        P(None, ("leaf", "agg")),
        P(None, ("leaf", "agg")),
        P(None, ("leaf", "agg")),
        P(),
        P(),
        P(),
        P(("leaf", "agg"), None, None),
        P(("leaf", "agg"), None, None),
        P(None, ("leaf", "agg")),
        P(("leaf", "agg")),
    )
    out_specs = (P("probe", None, ("leaf", "agg")), P("probe", None, ("leaf", "agg")), P())
    return jax.shard_map(
        on_device, mesh=mesh, in_specs=in_specs, out_specs=out_specs, check_vma=False
    )
```

```python
import functools
import jax
import jax.numpy as jnp
from jax import lax
from jax.experimental import pallas as pl
from jax.experimental.pallas import tpu as pltpu
from jax.sharding import PartitionSpec as P

MESH = pl.DeviceIdType.MESH
F32 = jnp.float32
BF16 = jnp.bfloat16
AXES = ("leaf", "agg", "probe")
RELAX = 0.6
CAP = 16
NT = (((1,), (1,)), ((), ()))
X = 4

PAIR = 2


def split(value):
    high = value.astype(BF16)
    return high, (value - high.astype(F32)).astype(BF16)


def dot(left, right):
    return jnp.dot(left, right, preferred_element_type=F32)


def dot_exact(left, right_pair):
    return dot(left, right_pair[0]) + dot(left, right_pair[1])


def dot_split(left, right_pair):
    left_high, left_low = split(left)
    return dot(left_high, right_pair[0]) + (
        dot(left_low, right_pair[0]) + dot(left_high, right_pair[1])
    )


def group_steps(probes):
    def hops(step):
        return -(min(step[0], probes - step[0]) + step[1] + min(step[2], X - step[2]))

    steps = [
        (y, z, x, core)
        for y in range(probes)
        for z in range(PAIR)
        for x in range(X)
        for core in range(2)
    ][1:]
    return sorted(steps, key=hops)


def kernel(
    parts,
    probes,
    probe_far,
    visc_far,
    fric_far,
    sens_far,
    misfit_far,
    grad_far,
    trace_far,
    modes_far,
    inv_far,
    ints_in,
    out,
    trace_out,
    probe_in,
    visc_in,
    fric_in,
    sens_in,
    grad,
    trace,
    modes,
    inv,
    weights_h,
    weights_l,
    modes_h,
    modes_l,
    modes_t_h,
    modes_t_l,
    inv_h,
    inv_l,
    scatter,
    scatter_two,
    gather,
    gather_two,
    adjacent,
    group_sum,
    group_spread,
    visc,
    fric,
    misfit,
    inv_diag,
    count,
    count_near,
    probe_sens,
    rhs,
    first_dir,
    image,
    pre,
    traces,
    home,
    moved,
    ints,
    result_out,
    result_in,
    send,
    recv,
    sums,
    sums_in,
    solved_own,
    solved,
    dots_a,
    dots_b,
    traces_all,
    send_sem,
    recv_sem,
    move_send_sem,
    move_recv_sem,
    coarse_send_sem,
    coarse_recv_sem,
    dots_send_sem,
    dots_recv_sem,
    last_send_sem,
    last_recv_sem,
    load_sem,
):
    loads = [
        pltpu.make_async_copy(far, near, load_sem.at[which])
        for which, (far, near) in enumerate(
            [
                (visc_far, visc_in),
                (grad_far, grad),
                (fric_far, fric_in),
                (trace_far, trace),
                (sens_far, sens_in),
                (probe_far, probe_in),
                (modes_far, modes),
                (inv_far, inv),
            ]
        )
    ]
    for load in loads:
        load.start()
    leaf, core, along = lax.axis_index("leaf"), lax.axis_index("agg"), lax.axis_index("probe")
    z, x = lax.div(leaf, X), lax.rem(leaf, X)
    probe, low = lax.div(z, PAIR), lax.rem(z, PAIR)
    unit = ((along * PAIR + low) * X + x) * 2 + core
    mirror_leaf = (along * PAIR + low) * X + x
    at_home = along == probe
    ndof = grad.shape[0]
    elems = visc_in.shape[1]
    slots = parts * CAP
    halves = CAP // 2
    others = parts - 1
    rest = 2 * elems - ndof

    lows = [lax.rem(low + step, PAIR) for step in range(PAIR)]
    xs = [lax.rem(x + step, X) for step in range(X)]
    cores = [core, 1 - core]
    alongs = [lax.rem(along + step, probes) for step in range(probes)]
    leaves = [[(probe * PAIR + part) * X + place for place in xs] for part in lows]

    def reached(step):
        y_step, z_step, x_step, core_step = step
        device = (leaves[z_step][x_step], cores[core_step], alongs[y_step])
        peer = ((alongs[y_step] * PAIR + lows[z_step]) * X + xs[x_step]) * 2 + cores[core_step]
        return device, peer

    steps = group_steps(probes)
    peers = [reached(step) for step in steps]
    inverse = {
        step: ((probes - step[0]) % probes, step[1], (X - step[2]) % X, step[3]) for step in steps
    }
    pair_steps = [
        step
        for step in steps
        if step == inverse[step]
        or (step < inverse[step]) == ((step[1] + step[3]) % 2 == 0)
    ]
    mates = [
        ((lax.rem(probe + step, probes) * PAIR + low) * X + x, core, along)
        for step in range(1, probes)
    ]
    mirrors = [(mirror_leaf, side, probe) for side in cores]

    barrier = pltpu.get_barrier_semaphore()
    for device in [device for device, _ in peers] + mates:
        pl.semaphore_signal(barrier, inc=1, device_id=device, device_id_type=MESH)

    @pl.when(jnp.logical_not(at_home))
    def _():
        for device in mirrors:
            pl.semaphore_signal(barrier, inc=1, device_id=device, device_id_type=MESH)

    def wait_bytes(ref, sem):
        pltpu.make_async_copy(ref, ref, sem).wait()

    def mirror_start(source, target, send_at, recv_at, step=0):
        def remote():
            return pltpu.make_async_remote_copy(
                src_ref=source,
                dst_ref=target,
                send_sem=send_at,
                recv_sem=recv_at,
                device_id=mirrors[step],
                device_id_type=MESH,
            )

        if step:
            remote().start()
        else:

            @pl.when(at_home)
            def _():
                pltpu.make_async_copy(source, target, recv_at).start()

            @pl.when(jnp.logical_not(at_home))
            def _():
                remote().start()

    def mirror_sent(source, send_at, step=0):
        if step:
            wait_bytes(source, send_at)
        else:

            @pl.when(jnp.logical_not(at_home))
            def _():
                wait_bytes(source, send_at)

    rows = lax.broadcasted_iota(jnp.int32, (elems, elems), 0).astype(F32)

    def one_hot(ref, row):
        return (ref[pl.ds(row, 1), :] == rows).astype(F32)

    base = slots // elems

    def adjacency(ref):
        ends = [one_hot(ref, base + end).astype(BF16) for end in range(2)]
        near = lax.dot_general(ends[0], ends[1], NT, preferred_element_type=F32)
        return near + lax.dot_general(ends[1], ends[0], NT, preferred_element_type=F32)

    def inverse_diagonal(visc_t, fric_t, counts):
        square = grad[...] * grad[...]
        trace_square = jnp.sum(trace[...] * trace[...], axis=0, keepdims=True)
        return RELAX / (dot_split(visc_t, split(square)) + fric_t + counts * trace_square)

    touching = jnp.zeros((elems, 1), F32)
    for block in range(base):
        touching = touching + jnp.sum(one_hot(ints_in, block), axis=1, keepdims=True)
    touching = touching + jnp.sum(adjacency(ints_in), axis=1, keepdims=True)
    for load in loads[:6]:
        load.wait()
    home_diag = inverse_diagonal(visc_in[...].T, fric_in[...].T, touching)
    home[...] = ((sens_in[...] * probe_in[0]).T * home_diag).T
    for turn in range(2):
        recv[turn, unit] = jnp.zeros(recv.shape[2:], F32)

    @pl.when(at_home)
    def _():
        pl.semaphore_wait(barrier, others + probes - 1)

    @pl.when(jnp.logical_not(at_home))
    def _():
        pl.semaphore_wait(barrier, others + probes + 1)

    sources = [ints_in, home, visc_in, fric_in, misfit_far]
    targets = [ints] + [moved.at[which] for which in range(4)]

    def moved_start(which):
        mirror_start(
            sources[which], targets[which], move_send_sem.at[which], move_recv_sem.at[which]
        )

    for which in range(4):
        moved_start(which)

    def moved_end(which):
        wait_bytes(targets[which], move_recv_sem.at[which])
        mirror_sent(sources[which], move_send_sem.at[which])

    for slot, matrix in enumerate((grad[...].T, grad[...], trace[...].T, trace[...])):
        weights_h[slot], weights_l[slot] = split(matrix)
    for load in loads[6:]:
        load.wait()
    modes_h[...], modes_l[...] = split(modes[...])
    modes_t_h[...], modes_t_l[...] = split(modes[...].T)
    for block in range(inv.shape[0]):
        inv_h[block], inv_l[block] = split(inv[block])
    moved_end(0)
    cross = jnp.zeros((elems, 1), F32)
    for block in range(base):
        hot = one_hot(ints, block)
        cross = cross + jnp.sum(hot, axis=1, keepdims=True)
        here = pl.ds(block * elems, elems)
        scatter[:, here] = hot.astype(BF16)
        hot_t = hot.T
        gather[here, :] = hot_t.astype(BF16)
        paired = hot_t.reshape(elems // CAP, 2, halves, elems)
        half = pl.ds(block * (elems // 2), elems // 2)
        gather_two[half, :elems] = paired[:, 0].reshape(elems // 2, elems).astype(BF16)
        gather_two[half, elems:] = paired[:, 1].reshape(elems // 2, elems).astype(BF16)
    for block in range(base // 2):
        here = pl.ds(block * elems, elems)
        scatter_two[:elems, here] = gather_two[here, :elems].astype(F32).T.astype(BF16)
        scatter_two[elems:, here] = gather_two[here, elems:].astype(F32).T.astype(BF16)
    near_pairs = adjacency(ints)
    adjacent[...] = near_pairs.astype(BF16)
    count_near[...] = jnp.sum(near_pairs, axis=1, keepdims=True)
    count[...] = cross + count_near[...]
    hot = one_hot(ints, base + 2)
    group_sum[...] = hot[: sums.shape[0]].astype(BF16)
    group_spread[...] = hot.T.astype(BF16)
    solved[...] = jnp.zeros_like(solved)
    moved_end(1)
    pre[...] = moved[0].T

    def weight(slot):
        return weights_h[slot], weights_l[slot]

    def wait_blocks(turn, sem, blocks=others):
        wait_bytes(recv.at[turn, pl.ds(0, blocks)], sem.at[turn])

    def send_traces(value, turn, receivers):
        traced = dot_split(value, weight(2))
        high, low_part = split(traced)
        blank = jnp.zeros((elems, rest), BF16)
        send[turn, :, :CAP, :] = dot_exact(
            gather[...], (high[:, :elems], low_part[:, :elems])
        ).reshape(parts, CAP, elems)

        def two(piece):
            tail = piece[:, elems:]
            return jnp.concatenate(
                [jnp.concatenate([tail, blank], 1), jnp.concatenate([blank, tail], 1)], 0
            )

        send[turn, :, CAP:, :] = dot_exact(
            gather_two[...], (two(high), two(low_part))
        ).reshape(parts, halves, elems)
        for device, peer in receivers:
            pltpu.make_async_remote_copy(
                src_ref=send.at[turn, peer],
                dst_ref=recv.at[turn, unit],
                send_sem=send_sem.at[turn],
                recv_sem=recv_sem.at[turn],
                device_id=device,
                device_id_type=MESH,
            ).start()
        return traced, high, low_part

    def energy(value, turn):
        traced, high, low_part = send_traces(value, turn, [reached(step) for step in pair_steps])
        strain = dot_split(value, weight(0))
        near = count_near[...] * traced - dot_exact(adjacent[...], (high, low_part))
        total = lanes(visc[...] * strain, strain)
        total = total + lanes(fric[...] * value, value) + lanes(near, traced)
        wait_blocks(turn, recv_sem, len(pair_steps))
        once = jnp.zeros(recv.shape[2:], F32)
        twice = jnp.zeros(recv.shape[2:], F32)
        for step in pair_steps:
            _, peer = reached(inverse[step])
            jump = send[turn, peer] - recv[turn, peer]
            if step == inverse[step]:
                twice = twice + jump * jump
            else:
                once = once + jump * jump
        wait_blocks(turn, send_sem, len(pair_steps))
        return total + jnp.sum(once + 0.5 * twice, axis=0, keepdims=True)

    def operate(value, turn, started=None):
        traced, high, low_part = send_traces(value, turn, peers)
        if started is not None:
            started()
        inner = dot_split(visc[...] * dot_split(value, weight(0)), weight(1))
        near = count[...] * traced - dot_exact(adjacent[...], (high, low_part))
        inner = inner + fric[...] * value
        wait_blocks(turn, recv_sem)
        first = dot_exact(scatter[...], split(recv[turn, :, :CAP, :].reshape(slots, elems)))
        second = dot_exact(
            scatter_two[...], split(recv[turn, :, CAP:, :].reshape(slots // 2, elems))
        )
        second = second[:elems, :rest] + second[elems:, rest:]
        near = near - jnp.concatenate([first, second], 1)
        result = inner + dot_split(near, weight(3))
        wait_blocks(turn, send_sem)
        return result

    own_aggs = inv.shape[0]

    def agg_rows(side):
        return pl.ds(pl.multiple_of(side * own_aggs, own_aggs), own_aggs)

    def coarse_start(residual):
        projected = dot_split(residual, (modes_h[...], modes_l[...]))
        sums[...] = dot_exact(group_sum[...], split(projected))
        for step, side in enumerate(cores):
            mirror_start(
                sums.at[agg_rows(side)],
                sums_in.at[step],
                coarse_send_sem.at[step],
                coarse_recv_sem.at[step],
                step,
            )

    def coarse_solve():
        for step, side in enumerate(cores):
            wait_bytes(sums_in.at[step], coarse_recv_sem.at[step])
            mirror_sent(sums.at[agg_rows(side)], coarse_send_sem.at[step], step)
        total = sums_in[0] + sums_in[1]
        row = lax.broadcasted_iota(jnp.int32, total.shape, 0)
        result = jnp.zeros_like(total)
        for block in range(own_aggs):
            one = dot_split(total, (inv_h[block], inv_l[block]))
            result = jnp.where(row == block, one, result)
        solved_own[...] = result
        for step in range(2):
            mirror_start(
                solved_own,
                solved.at[agg_rows(core)],
                coarse_send_sem.at[2 + step],
                coarse_recv_sem.at[2 + step],
                step,
            )

    def coarse_end():
        for step, side in enumerate(cores):
            wait_bytes(solved.at[agg_rows(side)], coarse_recv_sem.at[2 + step])
            mirror_sent(solved_own, coarse_send_sem.at[2 + step], step)
        spread = dot_exact(group_spread[...], split(solved[...]))
        return dot_split(spread, (modes_t_h[...], modes_t_l[...]))

    def precondition(residual_ref, turn, started, later=None):
        def beside():
            started()
            coarse_start(residual_ref[...])

        changed = operate(pre[...], turn, beside)
        pre[...] += (residual_ref[...] - changed) * inv_diag[...]
        coarse_solve()
        changed = operate(pre[...], 1 - turn, later)
        pre[...] += (residual_ref[...] - changed) * inv_diag[...]
        return pre[...] + coarse_end()

    def lanes(left, right):
        total = jnp.sum(left * right, axis=0, keepdims=True)
        tail = jnp.concatenate([total[:, elems:], jnp.zeros((1, rest), F32)], 1)
        return total[:, :elems] + tail

    stage_steps = [
        [step for step in steps if step[2:] == (0, 0)],
        [step for step in steps if step[:2] == (0, 0)],
    ]
    stage_spots = [along * PAIR + low, x * 2 + core]
    stage_buffers = [dots_a, dots_b]

    def dots_send(which, stage, row):
        spot = stage_buffers[stage].at[which, stage_spots[stage]]
        spot[...] = row
        for step in stage_steps[stage]:
            pltpu.make_async_remote_copy(
                src_ref=spot,
                dst_ref=spot,
                send_sem=dots_send_sem.at[which, stage],
                recv_sem=dots_recv_sem.at[which, stage],
                device_id=reached(step)[0],
                device_id_type=MESH,
            ).start()

    def dots_sum(which, stage):
        blocks = stage_buffers[stage].at[which, pl.ds(0, len(stage_steps[stage]))]
        wait_bytes(blocks, dots_recv_sem.at[which, stage])
        wait_bytes(blocks, dots_send_sem.at[which, stage])
        return jnp.sum(stage_buffers[stage][which], axis=0)

    def dots_start(which, pieces):
        column = jnp.concatenate(list(pieces) + [jnp.zeros((8 - len(pieces), elems), F32)], 0)
        column = jnp.sum(column, axis=1, keepdims=True)
        across = lax.broadcasted_iota(jnp.int32, (8, elems), 1)
        down = lax.broadcasted_iota(jnp.int32, (8, elems), 0)
        row = jnp.sum(jnp.where(across == down, column, 0.0), axis=0, keepdims=True)
        dots_send(which, 0, row)

    def dots_next(which):
        dots_send(which, 1, dots_sum(which, 0))

    def dots_end(which):
        total = dots_sum(which, 1)
        return [total[:, lane : lane + 1] for lane in range(8)]

    @pl.loop(0, 2)
    def _(solve):
        def first_time():
            @pl.when(solve == 0)
            def _():
                moved_end(2)
                visc[...] = moved[1].T
                moved_end(3)
                fric[...] = moved[2].T
                inv_diag[...] = inverse_diagonal(visc[...], fric[...], count[...])
                start = pre[...] / inv_diag[...]
                probe_sens[...] = start
                rhs[...] = start
                moved_start(4)

        first_dir[...] = precondition(rhs, 0, first_time)
        image[...] = operate(first_dir[...], 0)
        pre[...] = image[...] * inv_diag[...]

        def sums_first():
            dots_start(
                0, [lanes(rhs[...], first_dir[...]), lanes(first_dir[...], image[...])]
            )

        second = precondition(image, 1, sums_first, functools.partial(dots_next, 0))
        energy_now, curve, *_ = dots_end(0)
        step = energy_now / curve
        second = first_dir[...] - step * second
        residual = rhs[...] - step * image[...]
        pre[...] = second
        energy_second = energy(pre[...], 1)
        second = pre[...]
        dots_start(
            1,
            [
                lanes(residual, second),
                energy_second,
                lanes(second, image[...]),
                lanes(probe_sens[...], first_dir[...]),
                lanes(probe_sens[...], second),
            ],
        )

        @pl.when(solve == 0)
        def _():
            moved_end(4)
            misfit[...] = moved[3].T

        dots_next(1)
        energy_next, curve_zz, curve_zp, trace_first, trace_second, *_ = dots_end(1)
        ratio = energy_next / energy_now
        curve_next = curve_zz + 2.0 * ratio * curve_zp + ratio * ratio * curve
        step_next = energy_next / curve_next
        weight_first = step + step_next * ratio
        result = weight_first * first_dir[...] + step_next * pre[...]
        result_out[solve] = result.T
        mirror_start(
            result_out.at[solve],
            result_in.at[solve],
            move_send_sem.at[6 + solve],
            move_recv_sem.at[6 + solve],
        )
        source = misfit[...] * result
        rhs[...] = source
        pre[...] = source * inv_diag[...]
        value = weight_first * trace_first + step_next * trace_second
        traces[...] = jnp.broadcast_to(value, traces.shape)

    traces_all[probe] = traces[...]
    for device in mates:
        pltpu.make_async_remote_copy(
            src_ref=traces,
            dst_ref=traces_all.at[probe],
            send_sem=last_send_sem,
            recv_sem=last_recv_sem,
            device_id=device,
            device_id_type=MESH,
        ).start()
    for solve in range(2):
        wait_bytes(result_in.at[solve], move_recv_sem.at[6 + solve])
        mirror_sent(result_out.at[solve], move_send_sem.at[6 + solve])
    out[0] = result_in[0]
    out[1] = result_in[1] * sens_in[...]
    blocks = traces_all.at[pl.ds(0, probes - 1)]
    wait_bytes(blocks, last_recv_sem)
    wait_bytes(blocks, last_send_sem)
    trace_out[...] = jnp.sum(traces_all[...], axis=0) / probes


def on_device(
    probes,
    viscosity,
    friction,
    sensitivity,
    misfit_weight,
    grad_ref,
    trace_ref,
    coarse_modes,
    coarse_inv,
    peer_slots,
    local_pairs,
    elem_agg,
):
    leaves, aggs, count = (lax.axis_size(axis) for axis in AXES)
    parts = leaves * aggs
    ndof, elems = viscosity.shape
    own_aggs, modes_n = coarse_inv.shape[:2]
    slots = parts * CAP
    ints = jnp.concatenate(
        [
            peer_slots.reshape(slots // elems, elems),
            local_pairs,
            elem_agg[None],
            jnp.zeros((5, elems), jnp.int32),
        ]
    ).astype(F32)

    def vmem(*shape, dtype=F32):
        return pltpu.VMEM(shape, dtype)

    field = vmem(elems, ndof)
    block_rows = CAP + CAP // 2
    dma = pltpu.SemaphoreType.DMA
    scratch = [
        vmem(1, ndof, elems),
        vmem(ndof, elems),
        vmem(ndof, elems),
        vmem(ndof, elems),
        vmem(ndof, ndof),
        vmem(ndof, ndof),
        vmem(ndof, modes_n),
        vmem(own_aggs, modes_n, modes_n),
        vmem(4, ndof, ndof, dtype=BF16),
        vmem(4, ndof, ndof, dtype=BF16),
        vmem(ndof, modes_n, dtype=BF16),
        vmem(ndof, modes_n, dtype=BF16),
        vmem(modes_n, ndof, dtype=BF16),
        vmem(modes_n, ndof, dtype=BF16),
        vmem(own_aggs, modes_n, modes_n, dtype=BF16),
        vmem(own_aggs, modes_n, modes_n, dtype=BF16),
        vmem(elems, slots, dtype=BF16),
        vmem(2 * elems, slots // 2, dtype=BF16),
        vmem(slots, elems, dtype=BF16),
        vmem(slots // 2, 2 * elems, dtype=BF16),
        vmem(elems, elems, dtype=BF16),
        vmem(aggs * own_aggs, elems, dtype=BF16),
        vmem(elems, elems, dtype=BF16),
        field,
        field,
        field,
        field,
        vmem(elems, 1),
        vmem(elems, 1),
        field,
        field,
        field,
        field,
        field,
        vmem(8, elems),
        vmem(ndof, elems),
        vmem(4, ndof, elems),
        vmem(*ints.shape),
        vmem(2, ndof, elems),
        vmem(2, ndof, elems),
        vmem(2, parts, block_rows, elems),
        vmem(2, parts, block_rows, elems),
        vmem(aggs * own_aggs, modes_n),
        vmem(2, own_aggs, modes_n),
        vmem(own_aggs, modes_n),
        vmem(elems, modes_n),
        vmem(2, count * PAIR, 1, elems),
        vmem(2, 2 * X, 1, elems),
        vmem(count, 8, elems),
        dma((2,)),
        dma((2,)),
        dma((8,)),
        dma((8,)),
        dma((4,)),
        dma((4,)),
        dma((2, 2)),
        dma((2, 2)),
        dma,
        dma,
        dma((8,)),
    ]
    out, trace_tile = pl.pallas_call(
        functools.partial(kernel, parts, count),
        out_shape=(
            jax.ShapeDtypeStruct((2, ndof, elems), F32),
            jax.ShapeDtypeStruct((8, elems), F32),
        ),
        in_specs=[pl.BlockSpec(memory_space=pltpu.HBM)] * 9
        + [pl.BlockSpec(memory_space=pltpu.VMEM)],
        out_specs=(pl.BlockSpec(memory_space=pltpu.VMEM),) * 2,
        scratch_shapes=scratch,
        compiler_params=pltpu.CompilerParams(
            collective_id=0, has_side_effects=True, vmem_limit_bytes=60 * 1024 * 1024
        ),
    )(
        probes,
        viscosity,
        friction,
        sensitivity,
        misfit_weight,
        grad_ref,
        trace_ref,
        coarse_modes,
        coarse_inv,
        ints,
    )
    return out[0][None], out[1][None], trace_tile[0, 0]


def solution(mesh):
    in_specs = (
        P("probe", None, ("leaf", "agg")),
        P(None, ("leaf", "agg")),
        P(None, ("leaf", "agg")),
        P(None, ("leaf", "agg")),
        P(None, ("leaf", "agg")),
        P(),
        P(),
        P(),
        P(("leaf", "agg"), None, None),
        P(("leaf", "agg"), None, None),
        P(None, ("leaf", "agg")),
        P(("leaf", "agg")),
    )
    out_specs = (P("probe", None, ("leaf", "agg")), P("probe", None, ("leaf", "agg")), P())
    return jax.shard_map(
        on_device, mesh=mesh, in_specs=in_specs, out_specs=out_specs, check_vma=False
    )
```

```python
import functools
import jax
import jax.numpy as jnp
from jax import lax
from jax.experimental import pallas as pl
from jax.experimental.pallas import tpu as pltpu
from jax.sharding import PartitionSpec as P

MESH = pl.DeviceIdType.MESH
F32 = jnp.float32
BF16 = jnp.bfloat16
AXES = ("leaf", "agg", "probe")
RELAX = 0.6
CAP = 16
NT = (((1,), (1,)), ((), ()))
X = 4

PAIR = 2


def split(value):
    high = value.astype(BF16)
    return high, (value - high.astype(F32)).astype(BF16)


def dot(left, right):
    return jnp.dot(left, right, preferred_element_type=F32)


def dot_exact(left, right_pair):
    return dot(left, right_pair[0]) + dot(left, right_pair[1])


def dot_split(left, right_pair):
    left_high, left_low = split(left)
    return dot(left_high, right_pair[0]) + (
        dot(left_low, right_pair[0]) + dot(left_high, right_pair[1])
    )


def group_steps(probes):
    def hops(step):
        return -(min(step[0], probes - step[0]) + step[1] + min(step[2], X - step[2]))

    steps = [
        (y, z, x, core)
        for y in range(probes)
        for z in range(PAIR)
        for x in range(X)
        for core in range(2)
    ][1:]
    return sorted(steps, key=hops)


def kernel(
    parts,
    probes,
    probe_far,
    visc_far,
    fric_far,
    sens_far,
    misfit_far,
    grad_far,
    trace_far,
    modes_far,
    inv_far,
    ints_in,
    first_out,
    second_out,
    trace_out,
    probe_in,
    visc_in,
    fric_in,
    sens_in,
    grad,
    trace,
    modes,
    inv,
    weights_h,
    weights_l,
    modes_h,
    modes_l,
    modes_t_h,
    modes_t_l,
    inv_h,
    inv_l,
    scatter,
    scatter_two,
    gather,
    gather_two,
    adjacent,
    group_sum,
    group_spread,
    visc,
    fric,
    misfit,
    inv_diag,
    count,
    count_near,
    probe_sens,
    rhs,
    first_dir,
    image,
    pre,
    traces,
    home,
    moved,
    ints,
    result_out,
    result_in,
    send,
    recv,
    sums,
    sums_in,
    solved_own,
    solved,
    dots_a,
    dots_b,
    traces_all,
    send_sem,
    recv_sem,
    move_send_sem,
    move_recv_sem,
    coarse_send_sem,
    coarse_recv_sem,
    dots_send_sem,
    dots_recv_sem,
    last_send_sem,
    last_recv_sem,
    load_sem,
):
    loads = [
        pltpu.make_async_copy(far, near, load_sem.at[which])
        for which, (far, near) in enumerate(
            [
                (visc_far, visc_in),
                (grad_far, grad),
                (fric_far, fric_in),
                (trace_far, trace),
                (sens_far, sens_in),
                (probe_far, probe_in),
                (modes_far, modes),
                (inv_far, inv),
            ]
        )
    ]
    for load in loads:
        load.start()
    leaf, core, along = lax.axis_index("leaf"), lax.axis_index("agg"), lax.axis_index("probe")
    z, x = lax.div(leaf, X), lax.rem(leaf, X)
    probe, low = lax.div(z, PAIR), lax.rem(z, PAIR)
    quarter = lax.rem(along - probe + probes, probes)
    unit = ((quarter * PAIR + low) * X + x) * 2 + core
    at_home = along + probe == 0
    in_place = quarter == probe
    ndof = grad.shape[0]
    elems = visc_in.shape[1]
    slots = parts * CAP
    halves = CAP // 2
    others = parts - 1
    rest = 2 * elems - ndof

    lows = [lax.rem(low + step, PAIR) for step in range(PAIR)]
    xs = [lax.rem(x + step, X) for step in range(X)]
    cores = [core, 1 - core]
    alongs = [lax.rem(along + step, probes) for step in range(probes)]
    quarters = [lax.rem(quarter + step, probes) for step in range(probes)]
    leaves = [[(probe * PAIR + part) * X + place for place in xs] for part in lows]

    def reached(step):
        y_step, z_step, x_step, core_step = step
        device = (leaves[z_step][x_step], cores[core_step], alongs[y_step])
        peer = (quarters[y_step] * PAIR + lows[z_step]) * X + xs[x_step]
        peer = peer * 2 + cores[core_step]
        return device, peer

    steps = group_steps(probes)
    peers = [reached(step) for step in steps]
    inverse = {
        step: ((probes - step[0]) % probes, step[1], (X - step[2]) % X, step[3]) for step in steps
    }
    pair_steps = [
        step
        for step in steps
        if step == inverse[step]
        or (step < inverse[step]) == ((step[1] + step[3]) % 2 == 0)
    ]
    mates = [
        ((lax.rem(probe + step, probes) * PAIR + low) * X + x, core, along)
        for step in range(1, probes)
    ]
    away = (quarter * PAIR + low) * X + x
    homes = [(away, side, probe) for side in cores]
    workers = [
        ((along * PAIR + low) * X + x, side, lax.rem(probe + along, probes)) for side in cores
    ]
    plane = (away, core, along)

    barrier = pltpu.get_barrier_semaphore()
    for device in [device for device, _ in peers] + mates:
        pl.semaphore_signal(barrier, inc=1, device_id=device, device_id_type=MESH)

    @pl.when(jnp.logical_not(at_home))
    def _():
        for device in homes + workers:
            pl.semaphore_signal(barrier, inc=1, device_id=device, device_id_type=MESH)

    @pl.when(jnp.logical_not(in_place))
    def _():
        pl.semaphore_signal(barrier, inc=1, device_id=plane, device_id_type=MESH)

    def wait_bytes(ref, sem):
        pltpu.make_async_copy(ref, ref, sem).wait()

    def move_start(device, stays, source, target, send_at, recv_at):
        def remote():
            pltpu.make_async_remote_copy(
                src_ref=source,
                dst_ref=target,
                send_sem=send_at,
                recv_sem=recv_at,
                device_id=device,
                device_id_type=MESH,
            ).start()

        if stays is None:
            remote()
        else:

            @pl.when(stays)
            def _():
                pltpu.make_async_copy(source, target, recv_at).start()

            @pl.when(jnp.logical_not(stays))
            def _():
                remote()

    def move_sent(stays, source, send_at):
        if stays is None:
            wait_bytes(source, send_at)
        else:

            @pl.when(jnp.logical_not(stays))
            def _():
                wait_bytes(source, send_at)

    own_or_none = [at_home, None]

    rows = lax.broadcasted_iota(jnp.int32, (elems, elems), 0).astype(F32)

    def one_hot(ref, row):
        return (ref[pl.ds(row, 1), :] == rows).astype(F32)

    base = slots // elems

    def adjacency(ref):
        ends = [one_hot(ref, base + end).astype(BF16) for end in range(2)]
        near = lax.dot_general(ends[0], ends[1], NT, preferred_element_type=F32)
        return near + lax.dot_general(ends[1], ends[0], NT, preferred_element_type=F32)

    def inverse_diagonal(visc_t, fric_t, counts):
        square = grad[...] * grad[...]
        trace_square = jnp.sum(trace[...] * trace[...], axis=0, keepdims=True)
        return RELAX / (dot_split(visc_t, split(square)) + fric_t + counts * trace_square)

    touching = jnp.zeros((elems, 1), F32)
    for block in range(base):
        touching = touching + jnp.sum(one_hot(ints_in, block), axis=1, keepdims=True)
    touching = touching + jnp.sum(adjacency(ints_in), axis=1, keepdims=True)
    for load in loads[:6]:
        load.wait()
    home_diag = inverse_diagonal(visc_in[...].T, fric_in[...].T, touching)
    home[...] = ((sens_in[...] * probe_in[0]).T * home_diag).T
    for turn in range(2):
        recv[turn, unit] = jnp.zeros(recv.shape[2:], F32)

    @pl.when(at_home)
    def _():
        pl.semaphore_wait(barrier, others + probes - 1)

    @pl.when(jnp.logical_and(in_place, jnp.logical_not(at_home)))
    def _():
        pl.semaphore_wait(barrier, others + probes + 3)

    @pl.when(jnp.logical_not(in_place))
    def _():
        pl.semaphore_wait(barrier, others + probes + 4)

    sources = [ints_in, home, visc_in, fric_in, misfit_far]
    targets = [ints] + [moved.at[which] for which in range(4)]

    ways = [(plane, in_place), (workers[0], at_home)] + [(plane, in_place)] * 3

    def moved_start(which):
        device, stays = ways[which]
        move_start(
            device,
            stays,
            sources[which],
            targets[which],
            move_send_sem.at[which],
            move_recv_sem.at[which],
        )

    def moved_end(which):
        wait_bytes(targets[which], move_recv_sem.at[which])
        move_sent(ways[which][1], sources[which], move_send_sem.at[which])

    for which in range(4):
        moved_start(which)

    for slot, matrix in enumerate((grad[...].T, grad[...], trace[...].T, trace[...])):
        weights_h[slot], weights_l[slot] = split(matrix)
    for load in loads[6:]:
        load.wait()
    modes_h[...], modes_l[...] = split(modes[...])
    modes_t_h[...], modes_t_l[...] = split(modes[...].T)
    for block in range(inv.shape[0]):
        inv_h[block], inv_l[block] = split(inv[block])
    moved_end(0)
    cross = jnp.zeros((elems, 1), F32)
    for block in range(base):
        hot = one_hot(ints, block)
        cross = cross + jnp.sum(hot, axis=1, keepdims=True)
        here = pl.ds(block * elems, elems)
        scatter[:, here] = hot.astype(BF16)
        hot_t = hot.T
        gather[here, :] = hot_t.astype(BF16)
        paired = hot_t.reshape(elems // CAP, 2, halves, elems)
        half = pl.ds(block * (elems // 2), elems // 2)
        gather_two[half, :elems] = paired[:, 0].reshape(elems // 2, elems).astype(BF16)
        gather_two[half, elems:] = paired[:, 1].reshape(elems // 2, elems).astype(BF16)
    for block in range(base // 2):
        here = pl.ds(block * elems, elems)
        scatter_two[:elems, here] = gather_two[here, :elems].astype(F32).T.astype(BF16)
        scatter_two[elems:, here] = gather_two[here, elems:].astype(F32).T.astype(BF16)
    near_pairs = adjacency(ints)
    adjacent[...] = near_pairs.astype(BF16)
    count_near[...] = jnp.sum(near_pairs, axis=1, keepdims=True)
    count[...] = cross + count_near[...]
    hot = one_hot(ints, base + 2)
    group_sum[...] = hot[: sums.shape[0]].astype(BF16)
    group_spread[...] = hot.T.astype(BF16)
    solved[...] = jnp.zeros_like(solved)
    moved_end(1)
    pre[...] = moved[0].T

    def weight(slot):
        return weights_h[slot], weights_l[slot]

    def wait_blocks(turn, sem, blocks=others):
        wait_bytes(recv.at[turn, pl.ds(0, blocks)], sem.at[turn])

    def send_traces(value, turn, receivers):
        traced = dot_split(value, weight(2))
        high, low_part = split(traced)
        blank = jnp.zeros((elems, rest), BF16)
        send[turn, :, :CAP, :] = dot_exact(
            gather[...], (high[:, :elems], low_part[:, :elems])
        ).reshape(parts, CAP, elems)

        def two(piece):
            tail = piece[:, elems:]
            return jnp.concatenate(
                [jnp.concatenate([tail, blank], 1), jnp.concatenate([blank, tail], 1)], 0
            )

        send[turn, :, CAP:, :] = dot_exact(
            gather_two[...], (two(high), two(low_part))
        ).reshape(parts, halves, elems)
        for device, peer in receivers:
            pltpu.make_async_remote_copy(
                src_ref=send.at[turn, peer],
                dst_ref=recv.at[turn, unit],
                send_sem=send_sem.at[turn],
                recv_sem=recv_sem.at[turn],
                device_id=device,
                device_id_type=MESH,
            ).start()
        return traced, high, low_part

    def energy(value, turn):
        traced, high, low_part = send_traces(value, turn, [reached(step) for step in pair_steps])
        strain = dot_split(value, weight(0))
        near = count_near[...] * traced - dot_exact(adjacent[...], (high, low_part))
        total = lanes(visc[...] * strain, strain)
        total = total + lanes(fric[...] * value, value) + lanes(near, traced)
        wait_blocks(turn, recv_sem, len(pair_steps))
        once = jnp.zeros(recv.shape[2:], F32)
        twice = jnp.zeros(recv.shape[2:], F32)
        for step in pair_steps:
            _, peer = reached(inverse[step])
            jump = send[turn, peer] - recv[turn, peer]
            if step == inverse[step]:
                twice = twice + jump * jump
            else:
                once = once + jump * jump
        wait_blocks(turn, send_sem, len(pair_steps))
        return total + jnp.sum(once + 0.5 * twice, axis=0, keepdims=True)

    def operate(value, turn, started=None):
        traced, high, low_part = send_traces(value, turn, peers)
        if started is not None:
            started()
        inner = dot_split(visc[...] * dot_split(value, weight(0)), weight(1))
        near = count[...] * traced - dot_exact(adjacent[...], (high, low_part))
        inner = inner + fric[...] * value
        wait_blocks(turn, recv_sem)
        first = dot_exact(scatter[...], split(recv[turn, :, :CAP, :].reshape(slots, elems)))
        second = dot_exact(
            scatter_two[...], split(recv[turn, :, CAP:, :].reshape(slots // 2, elems))
        )
        second = second[:elems, :rest] + second[elems:, rest:]
        near = near - jnp.concatenate([first, second], 1)
        result = inner + dot_split(near, weight(3))
        wait_blocks(turn, send_sem)
        return result

    own_aggs = inv.shape[0]

    def agg_rows(side):
        return pl.ds(pl.multiple_of(side * own_aggs, own_aggs), own_aggs)

    def coarse_start(residual):
        projected = dot_split(residual, (modes_h[...], modes_l[...]))
        sums[...] = dot_exact(group_sum[...], split(projected))
        for step, side in enumerate(cores):
            move_start(
                homes[step],
                own_or_none[step],
                sums.at[agg_rows(side)],
                sums_in.at[step],
                coarse_send_sem.at[step],
                coarse_recv_sem.at[step],
            )

    def coarse_solve():
        for step, side in enumerate(cores):
            wait_bytes(sums_in.at[step], coarse_recv_sem.at[step])
            move_sent(own_or_none[step], sums.at[agg_rows(side)], coarse_send_sem.at[step])
        total = sums_in[0] + sums_in[1]
        row = lax.broadcasted_iota(jnp.int32, total.shape, 0)
        result = jnp.zeros_like(total)
        for block in range(own_aggs):
            one = dot_split(total, (inv_h[block], inv_l[block]))
            result = jnp.where(row == block, one, result)
        solved_own[...] = result
        for step in range(2):
            move_start(
                workers[step],
                own_or_none[step],
                solved_own,
                solved.at[agg_rows(core)],
                coarse_send_sem.at[2 + step],
                coarse_recv_sem.at[2 + step],
            )

    def coarse_end():
        for step, side in enumerate(cores):
            wait_bytes(solved.at[agg_rows(side)], coarse_recv_sem.at[2 + step])
            move_sent(own_or_none[step], solved_own, coarse_send_sem.at[2 + step])
        spread = dot_exact(group_spread[...], split(solved[...]))
        return dot_split(spread, (modes_t_h[...], modes_t_l[...]))

    def precondition(residual_ref, turn, started, later=None):
        def beside():
            started()
            coarse_solve()

        changed = operate(pre[...], turn, beside)
        pre[...] += (residual_ref[...] - changed) * inv_diag[...]
        changed = operate(pre[...], 1 - turn, later)
        pre[...] += (residual_ref[...] - changed) * inv_diag[...]
        return pre[...] + coarse_end()

    def lanes(left, right):
        total = jnp.sum(left * right, axis=0, keepdims=True)
        tail = jnp.concatenate([total[:, elems:], jnp.zeros((1, rest), F32)], 1)
        return total[:, :elems] + tail

    stage_steps = [
        [step for step in steps if step[2:] == (0, 0)],
        [step for step in steps if step[:2] == (0, 0)],
    ]
    stage_spots = [quarter * PAIR + low, x * 2 + core]
    stage_buffers = [dots_a, dots_b]

    def dots_send(which, stage, row):
        spot = stage_buffers[stage].at[which, stage_spots[stage]]
        spot[...] = row
        for step in stage_steps[stage]:
            pltpu.make_async_remote_copy(
                src_ref=spot,
                dst_ref=spot,
                send_sem=dots_send_sem.at[which, stage],
                recv_sem=dots_recv_sem.at[which, stage],
                device_id=reached(step)[0],
                device_id_type=MESH,
            ).start()

    def dots_sum(which, stage):
        blocks = stage_buffers[stage].at[which, pl.ds(0, len(stage_steps[stage]))]
        wait_bytes(blocks, dots_recv_sem.at[which, stage])
        wait_bytes(blocks, dots_send_sem.at[which, stage])
        return jnp.sum(stage_buffers[stage][which], axis=0)

    def dots_start(which, pieces):
        column = jnp.concatenate(list(pieces) + [jnp.zeros((8 - len(pieces), elems), F32)], 0)
        column = jnp.sum(column, axis=1, keepdims=True)
        across = lax.broadcasted_iota(jnp.int32, (8, elems), 1)
        down = lax.broadcasted_iota(jnp.int32, (8, elems), 0)
        row = jnp.sum(jnp.where(across == down, column, 0.0), axis=0, keepdims=True)
        dots_send(which, 0, row)

    def dots_next(which):
        dots_send(which, 1, dots_sum(which, 0))

    def dots_end(which):
        total = dots_sum(which, 1)
        return [total[:, lane : lane + 1] for lane in range(8)]

    @pl.loop(0, 2)
    def _(solve):
        def first_time():
            @pl.when(solve == 0)
            def _():
                moved_end(2)
                visc[...] = moved[1].T
                moved_end(3)
                fric[...] = moved[2].T
                inv_diag[...] = inverse_diagonal(visc[...], fric[...], count[...])
                start = pre[...] / inv_diag[...]
                probe_sens[...] = start
                rhs[...] = start
                coarse_start(start)
                moved_start(4)

        @pl.when(solve != 0)
        def _():
            coarse_start(rhs[...])

        first_dir[...] = precondition(rhs, 0, first_time)
        image[...] = operate(first_dir[...], 0)
        pre[...] = image[...] * inv_diag[...]
        coarse_start(image[...])

        def sums_first():
            dots_start(
                0, [lanes(rhs[...], first_dir[...]), lanes(first_dir[...], image[...])]
            )

        second = precondition(image, 1, sums_first, functools.partial(dots_next, 0))
        energy_now, curve, *_ = dots_end(0)
        step = energy_now / curve
        second = first_dir[...] - step * second
        residual = rhs[...] - step * image[...]
        pre[...] = second
        energy_second = energy(pre[...], 1)
        second = pre[...]
        dots_start(
            1,
            [
                lanes(residual, second),
                energy_second,
                lanes(second, image[...]),
                lanes(probe_sens[...], first_dir[...]),
                lanes(probe_sens[...], second),
            ],
        )

        @pl.when(solve == 0)
        def _():
            moved_end(4)
            misfit[...] = moved[3].T

        dots_next(1)
        energy_next, curve_zz, curve_zp, trace_first, trace_second, *_ = dots_end(1)
        ratio = energy_next / energy_now
        curve_next = curve_zz + 2.0 * ratio * curve_zp + ratio * ratio * curve
        step_next = energy_next / curve_next
        weight_first = step + step_next * ratio
        result = weight_first * first_dir[...] + step_next * pre[...]
        result_out[solve] = result.T
        move_start(
            homes[0],
            at_home,
            result_out.at[solve],
            result_in.at[solve],
            move_send_sem.at[6 + solve],
            move_recv_sem.at[6 + solve],
        )
        source = misfit[...] * result
        rhs[...] = source
        pre[...] = source * inv_diag[...]
        value = weight_first * trace_first + step_next * trace_second
        traces[...] = jnp.broadcast_to(value, traces.shape)

    traces_all[probe] = traces[...]
    for device in mates:
        pltpu.make_async_remote_copy(
            src_ref=traces,
            dst_ref=traces_all.at[probe],
            send_sem=last_send_sem,
            recv_sem=last_recv_sem,
            device_id=device,
            device_id_type=MESH,
        ).start()
    for solve in range(2):
        wait_bytes(result_in.at[solve], move_recv_sem.at[6 + solve])
        move_sent(at_home, result_out.at[solve], move_send_sem.at[6 + solve])
    first_out[0] = result_in[0]
    second_out[0] = result_in[1] * sens_in[...]
    blocks = traces_all.at[pl.ds(0, probes - 1)]
    wait_bytes(blocks, last_recv_sem)
    wait_bytes(blocks, last_send_sem)
    trace_out[...] = jnp.sum(traces_all[...], axis=0) / probes


def on_device(
    probes,
    viscosity,
    friction,
    sensitivity,
    misfit_weight,
    grad_ref,
    trace_ref,
    coarse_modes,
    coarse_inv,
    peer_slots,
    local_pairs,
    elem_agg,
):
    leaves, aggs, count = (lax.axis_size(axis) for axis in AXES)
    parts = leaves * aggs
    ndof, elems = viscosity.shape
    own_aggs, modes_n = coarse_inv.shape[:2]
    slots = parts * CAP
    ints = jnp.concatenate(
        [
            peer_slots.reshape(slots // elems, elems),
            local_pairs,
            elem_agg[None],
            jnp.zeros((5, elems), jnp.int32),
        ]
    ).astype(F32)

    def vmem(*shape, dtype=F32):
        return pltpu.VMEM(shape, dtype)

    field = vmem(elems, ndof)
    block_rows = CAP + CAP // 2
    dma = pltpu.SemaphoreType.DMA
    scratch = [
        vmem(1, ndof, elems),
        vmem(ndof, elems),
        vmem(ndof, elems),
        vmem(ndof, elems),
        vmem(ndof, ndof),
        vmem(ndof, ndof),
        vmem(ndof, modes_n),
        vmem(own_aggs, modes_n, modes_n),
        vmem(4, ndof, ndof, dtype=BF16),
        vmem(4, ndof, ndof, dtype=BF16),
        vmem(ndof, modes_n, dtype=BF16),
        vmem(ndof, modes_n, dtype=BF16),
        vmem(modes_n, ndof, dtype=BF16),
        vmem(modes_n, ndof, dtype=BF16),
        vmem(own_aggs, modes_n, modes_n, dtype=BF16),
        vmem(own_aggs, modes_n, modes_n, dtype=BF16),
        vmem(elems, slots, dtype=BF16),
        vmem(2 * elems, slots // 2, dtype=BF16),
        vmem(slots, elems, dtype=BF16),
        vmem(slots // 2, 2 * elems, dtype=BF16),
        vmem(elems, elems, dtype=BF16),
        vmem(aggs * own_aggs, elems, dtype=BF16),
        vmem(elems, elems, dtype=BF16),
        field,
        field,
        field,
        field,
        vmem(elems, 1),
        vmem(elems, 1),
        field,
        field,
        field,
        field,
        field,
        vmem(8, elems),
        vmem(ndof, elems),
        vmem(4, ndof, elems),
        vmem(*ints.shape),
        vmem(2, ndof, elems),
        vmem(2, ndof, elems),
        vmem(2, parts, block_rows, elems),
        vmem(2, parts, block_rows, elems),
        vmem(aggs * own_aggs, modes_n),
        vmem(2, own_aggs, modes_n),
        vmem(own_aggs, modes_n),
        vmem(elems, modes_n),
        vmem(2, count * PAIR, 1, elems),
        vmem(2, 2 * X, 1, elems),
        vmem(count, 8, elems),
        dma((2,)),
        dma((2,)),
        dma((8,)),
        dma((8,)),
        dma((4,)),
        dma((4,)),
        dma((2, 2)),
        dma((2, 2)),
        dma,
        dma,
        dma((8,)),
    ]
    field_out = jax.ShapeDtypeStruct((1, ndof, elems), F32)
    first, second, trace_tile = pl.pallas_call(
        functools.partial(kernel, parts, count),
        out_shape=(
            field_out,
            field_out,
            jax.ShapeDtypeStruct((8, elems), F32),
        ),
        in_specs=[pl.BlockSpec(memory_space=pltpu.HBM)] * 9
        + [pl.BlockSpec(memory_space=pltpu.VMEM)],
        out_specs=(pl.BlockSpec(memory_space=pltpu.VMEM),) * 3,
        scratch_shapes=scratch,
        compiler_params=pltpu.CompilerParams(
            collective_id=0, has_side_effects=True, vmem_limit_bytes=60 * 1024 * 1024
        ),
    )(
        probes,
        viscosity,
        friction,
        sensitivity,
        misfit_weight,
        grad_ref,
        trace_ref,
        coarse_modes,
        coarse_inv,
        ints,
    )
    return first, second, trace_tile[0, 0]


def solution(mesh):
    in_specs = (
        P("probe", None, ("leaf", "agg")),
        P(None, ("leaf", "agg")),
        P(None, ("leaf", "agg")),
        P(None, ("leaf", "agg")),
        P(None, ("leaf", "agg")),
        P(),
        P(),
        P(),
        P(("leaf", "agg"), None, None),
        P(("leaf", "agg"), None, None),
        P(None, ("leaf", "agg")),
        P(("leaf", "agg")),
    )
    out_specs = (P("probe", None, ("leaf", "agg")), P("probe", None, ("leaf", "agg")), P())
    return jax.shard_map(
        on_device, mesh=mesh, in_specs=in_specs, out_specs=out_specs, check_vma=False
    )
```

```python
import functools
import jax
import jax.numpy as jnp
from jax import lax
from jax.experimental import pallas as pl
from jax.experimental.pallas import tpu as pltpu
from jax.sharding import PartitionSpec as P

MESH = pl.DeviceIdType.MESH
F32 = jnp.float32
BF16 = jnp.bfloat16
AXES = ("leaf", "agg", "probe")
RELAX = 0.6
CAP = 16
NT = (((1,), (1,)), ((), ()))
X = 4

PAIR = 2


def split(value):
    high = value.astype(BF16)
    return high, (value - high.astype(F32)).astype(BF16)


def dot(left, right):
    return jnp.dot(left, right, preferred_element_type=F32)


def dot_exact(left, right_pair):
    return dot(left, right_pair[0]) + dot(left, right_pair[1])


def dot_wide(left, right):
    width = right.shape[1]
    both = dot(left, jnp.concatenate(split(right), 1))
    return both[:, :width] + both[:, width:]


def dot_split(left, right_pair):
    left_high, left_low = split(left)
    return dot(left_high, right_pair[0]) + (
        dot(left_low, right_pair[0]) + dot(left_high, right_pair[1])
    )


def group_steps(probes):
    def hops(step):
        return -(min(step[0], probes - step[0]) + step[1] + min(step[2], X - step[2]))

    steps = [
        (y, z, x, core)
        for y in range(probes)
        for z in range(PAIR)
        for x in range(X)
        for core in range(2)
    ][1:]
    return sorted(steps, key=hops)


def kernel(
    parts,
    probes,
    probe_far,
    visc_far,
    fric_far,
    sens_far,
    misfit_far,
    grad_far,
    trace_far,
    modes_far,
    inv_far,
    ints_in,
    first_out,
    second_out,
    trace_out,
    probe_in,
    visc_in,
    fric_in,
    sens_in,
    grad,
    trace,
    modes,
    inv,
    weights_h,
    weights_l,
    modes_h,
    modes_l,
    modes_t_h,
    modes_t_l,
    inv_h,
    inv_l,
    scatter,
    scatter_two,
    gather,
    gather_two,
    adjacent,
    group_sum,
    group_spread,
    visc,
    fric,
    misfit,
    inv_diag,
    count,
    count_near,
    probe_sens,
    rhs,
    first_dir,
    image,
    pre,
    traces,
    home,
    moved,
    ints,
    result_out,
    result_in,
    send,
    recv,
    sums,
    sums_in,
    solved_own,
    solved,
    dots_a,
    dots_b,
    traces_all,
    send_sem,
    recv_sem,
    move_send_sem,
    move_recv_sem,
    coarse_send_sem,
    coarse_recv_sem,
    dots_send_sem,
    dots_recv_sem,
    last_send_sem,
    last_recv_sem,
    load_sem,
):
    loads = [
        pltpu.make_async_copy(far, near, load_sem.at[which])
        for which, (far, near) in enumerate(
            [
                (visc_far, visc_in),
                (grad_far, grad),
                (fric_far, fric_in),
                (trace_far, trace),
                (sens_far, sens_in),
                (probe_far, probe_in),
                (modes_far, modes),
                (inv_far, inv),
            ]
        )
    ]
    for load in loads:
        load.start()
    leaf, core, along = lax.axis_index("leaf"), lax.axis_index("agg"), lax.axis_index("probe")
    z, x = lax.div(leaf, X), lax.rem(leaf, X)
    probe, low = lax.div(z, PAIR), lax.rem(z, PAIR)
    quarter = lax.rem(along - probe + probes, probes)
    unit = ((quarter * PAIR + low) * X + x) * 2 + core
    at_home = along + probe == 0
    in_place = quarter == probe
    ndof = grad.shape[0]
    elems = visc_in.shape[1]
    slots = parts * CAP
    halves = CAP // 2
    others = parts - 1
    rest = 2 * elems - ndof

    lows = [lax.rem(low + step, PAIR) for step in range(PAIR)]
    xs = [lax.rem(x + step, X) for step in range(X)]
    cores = [core, 1 - core]
    alongs = [lax.rem(along + step, probes) for step in range(probes)]
    quarters = [lax.rem(quarter + step, probes) for step in range(probes)]
    leaves = [[(probe * PAIR + part) * X + place for place in xs] for part in lows]

    def reached(step):
        y_step, z_step, x_step, core_step = step
        device = (leaves[z_step][x_step], cores[core_step], alongs[y_step])
        peer = (quarters[y_step] * PAIR + lows[z_step]) * X + xs[x_step]
        peer = peer * 2 + cores[core_step]
        return device, peer

    steps = group_steps(probes)
    peers = [reached(step) for step in steps]
    inverse = {
        step: ((probes - step[0]) % probes, step[1], (X - step[2]) % X, step[3]) for step in steps
    }
    pair_steps = [
        step
        for step in steps
        if step == inverse[step]
        or (step < inverse[step]) == ((step[1] + step[3]) % 2 == 0)
    ]
    mates = [
        ((lax.rem(probe + step, probes) * PAIR + low) * X + x, core, along)
        for step in range(1, probes)
    ]
    away = (quarter * PAIR + low) * X + x
    homes = [(away, side, probe) for side in cores]
    workers = [
        ((along * PAIR + low) * X + x, side, lax.rem(probe + along, probes)) for side in cores
    ]
    plane = (away, core, along)

    barrier = pltpu.get_barrier_semaphore()
    for device in [device for device, _ in peers] + mates:
        pl.semaphore_signal(barrier, inc=1, device_id=device, device_id_type=MESH)

    @pl.when(jnp.logical_not(at_home))
    def _():
        for device in homes + workers:
            pl.semaphore_signal(barrier, inc=1, device_id=device, device_id_type=MESH)

    @pl.when(jnp.logical_not(in_place))
    def _():
        pl.semaphore_signal(barrier, inc=1, device_id=plane, device_id_type=MESH)

    def wait_bytes(ref, sem):
        pltpu.make_async_copy(ref, ref, sem).wait()

    def move_start(device, stays, source, target, send_at, recv_at):
        def remote():
            pltpu.make_async_remote_copy(
                src_ref=source,
                dst_ref=target,
                send_sem=send_at,
                recv_sem=recv_at,
                device_id=device,
                device_id_type=MESH,
            ).start()

        if stays is None:
            remote()
        else:

            @pl.when(stays)
            def _():
                pltpu.make_async_copy(source, target, recv_at).start()

            @pl.when(jnp.logical_not(stays))
            def _():
                remote()

    def move_sent(stays, source, send_at):
        if stays is None:
            wait_bytes(source, send_at)
        else:

            @pl.when(jnp.logical_not(stays))
            def _():
                wait_bytes(source, send_at)

    own_or_none = [at_home, None]

    rows = lax.broadcasted_iota(jnp.int32, (elems, elems), 0).astype(F32)

    def one_hot(ref, row):
        return (ref[pl.ds(row, 1), :] == rows).astype(F32)

    base = slots // elems

    def adjacency(ref):
        ends = [one_hot(ref, base + end).astype(BF16) for end in range(2)]
        near = lax.dot_general(ends[0], ends[1], NT, preferred_element_type=F32)
        return near + lax.dot_general(ends[1], ends[0], NT, preferred_element_type=F32)

    def inverse_diagonal(visc_t, fric_t, counts):
        square = grad[...] * grad[...]
        trace_square = jnp.sum(trace[...] * trace[...], axis=0, keepdims=True)
        return RELAX / (dot_split(visc_t, split(square)) + fric_t + counts * trace_square)

    touching = jnp.zeros((elems, 1), F32)
    for block in range(base):
        touching = touching + jnp.sum(one_hot(ints_in, block), axis=1, keepdims=True)
    touching = touching + jnp.sum(adjacency(ints_in), axis=1, keepdims=True)
    for load in loads[:6]:
        load.wait()
    home_diag = inverse_diagonal(visc_in[...].T, fric_in[...].T, touching)
    home[...] = ((sens_in[...] * probe_in[0]).T * home_diag).T
    for turn in range(2):
        recv[turn, unit] = jnp.zeros(recv.shape[2:], F32)

    @pl.when(at_home)
    def _():
        pl.semaphore_wait(barrier, others + probes - 1)

    @pl.when(jnp.logical_and(in_place, jnp.logical_not(at_home)))
    def _():
        pl.semaphore_wait(barrier, others + probes + 3)

    @pl.when(jnp.logical_not(in_place))
    def _():
        pl.semaphore_wait(barrier, others + probes + 4)

    sources = [ints_in, home, visc_in, fric_in, misfit_far]
    targets = [ints] + [moved.at[which] for which in range(4)]

    ways = [(plane, in_place), (workers[0], at_home)] + [(plane, in_place)] * 3

    def moved_start(which):
        device, stays = ways[which]
        move_start(
            device,
            stays,
            sources[which],
            targets[which],
            move_send_sem.at[which],
            move_recv_sem.at[which],
        )

    def moved_end(which):
        wait_bytes(targets[which], move_recv_sem.at[which])
        move_sent(ways[which][1], sources[which], move_send_sem.at[which])

    for which in range(4):
        moved_start(which)

    for slot, matrix in enumerate((grad[...].T, grad[...], trace[...].T, trace[...])):
        weights_h[slot], weights_l[slot] = split(matrix)
    for load in loads[6:]:
        load.wait()
    modes_h[...], modes_l[...] = split(modes[...])
    modes_t_h[...], modes_t_l[...] = split(modes[...].T)
    for block in range(inv.shape[0]):
        inv_h[block], inv_l[block] = split(inv[block])
    moved_end(0)
    cross = jnp.zeros((elems, 1), F32)
    for block in range(base):
        hot = one_hot(ints, block)
        cross = cross + jnp.sum(hot, axis=1, keepdims=True)
        here = pl.ds(block * elems, elems)
        scatter[:, here] = hot.astype(BF16)
        hot_t = hot.T
        gather[here, :elems] = hot_t.astype(BF16)
        gather[here, elems:] = hot_t.astype(BF16)
        paired = hot_t.reshape(elems // CAP, 2, halves, elems)
        half = pl.ds(block * (elems // 2), elems // 2)
        gather_two[half, :elems] = paired[:, 0].reshape(elems // 2, elems).astype(BF16)
        gather_two[half, elems:] = paired[:, 1].reshape(elems // 2, elems).astype(BF16)
    for block in range(base // 2):
        here = pl.ds(block * elems, elems)
        scatter_two[:elems, here] = gather_two[here, :elems].astype(F32).T.astype(BF16)
        scatter_two[elems:, here] = gather_two[here, elems:].astype(F32).T.astype(BF16)
    near_pairs = adjacency(ints)
    adjacent[...] = near_pairs.astype(BF16)
    count_near[...] = jnp.sum(near_pairs, axis=1, keepdims=True)
    count[...] = cross + count_near[...]
    hot = one_hot(ints, base + 2)
    group_sum[...] = hot[: sums.shape[0]].astype(BF16)
    group_spread[...] = hot.T.astype(BF16)
    solved[...] = jnp.zeros_like(solved)
    moved_end(1)
    pre[...] = moved[0].T

    def weight(slot):
        return weights_h[slot], weights_l[slot]

    def wait_blocks(turn, sem, blocks=others):
        wait_bytes(recv.at[turn, pl.ds(0, blocks)], sem.at[turn])

    def send_traces(value, turn, receivers):
        traced = dot_split(value, weight(2))
        high, low_part = split(traced)
        blank = jnp.zeros((elems, rest), BF16)
        both = jnp.concatenate([high[:, :elems], low_part[:, :elems]], 0)
        send[turn, :, :CAP, :] = dot(gather[...], both).reshape(parts, CAP, elems)

        def two(piece):
            tail = piece[:, elems:]
            return jnp.concatenate(
                [jnp.concatenate([tail, blank], 1), jnp.concatenate([blank, tail], 1)], 0
            )

        send[turn, :, CAP:, :] = dot_exact(
            gather_two[...], (two(high), two(low_part))
        ).reshape(parts, halves, elems)
        for device, peer in receivers:
            pltpu.make_async_remote_copy(
                src_ref=send.at[turn, peer],
                dst_ref=recv.at[turn, unit],
                send_sem=send_sem.at[turn],
                recv_sem=recv_sem.at[turn],
                device_id=device,
                device_id_type=MESH,
            ).start()
        return traced, high, low_part

    def energy(value, turn):
        traced, high, low_part = send_traces(value, turn, [reached(step) for step in pair_steps])
        strain = dot_split(value, weight(0))
        near = count_near[...] * traced - dot_exact(adjacent[...], (high, low_part))
        total = lanes(visc[...] * strain, strain)
        total = total + lanes(fric[...] * value, value) + lanes(near, traced)
        wait_blocks(turn, recv_sem, len(pair_steps))
        once = jnp.zeros(recv.shape[2:], F32)
        twice = jnp.zeros(recv.shape[2:], F32)
        for step in pair_steps:
            _, peer = reached(inverse[step])
            jump = send[turn, peer] - recv[turn, peer]
            if step == inverse[step]:
                twice = twice + jump * jump
            else:
                once = once + jump * jump
        wait_blocks(turn, send_sem, len(pair_steps))
        return total + jnp.sum(once + 0.5 * twice, axis=0, keepdims=True)

    def operate(value, turn, started=None):
        traced, high, low_part = send_traces(value, turn, peers)
        if started is not None:
            started()
        inner = dot_split(visc[...] * dot_split(value, weight(0)), weight(1))
        near = count[...] * traced - dot_exact(adjacent[...], (high, low_part))
        inner = inner + fric[...] * value
        wait_blocks(turn, recv_sem)
        first = dot_wide(scatter[...], recv[turn, :, :CAP, :].reshape(slots, elems))
        second = dot_wide(scatter_two[...], recv[turn, :, CAP:, :].reshape(slots // 2, elems))
        second = second[:elems, :rest] + second[elems:, rest:]
        near = near - jnp.concatenate([first, second], 1)
        result = inner + dot_split(near, weight(3))
        wait_blocks(turn, send_sem)
        return result

    own_aggs = inv.shape[0]

    def agg_rows(side):
        return pl.ds(pl.multiple_of(side * own_aggs, own_aggs), own_aggs)

    def coarse_start(residual):
        projected = dot_split(residual, (modes_h[...], modes_l[...]))
        sums[...] = dot_exact(group_sum[...], split(projected))
        for step, side in enumerate(cores):
            move_start(
                homes[step],
                own_or_none[step],
                sums.at[agg_rows(side)],
                sums_in.at[step],
                coarse_send_sem.at[step],
                coarse_recv_sem.at[step],
            )

    def coarse_solve():
        for step, side in enumerate(cores):
            wait_bytes(sums_in.at[step], coarse_recv_sem.at[step])
            move_sent(own_or_none[step], sums.at[agg_rows(side)], coarse_send_sem.at[step])
        total = sums_in[0] + sums_in[1]
        row = lax.broadcasted_iota(jnp.int32, total.shape, 0)
        result = jnp.zeros_like(total)
        for block in range(own_aggs):
            one = dot_split(total, (inv_h[block], inv_l[block]))
            result = jnp.where(row == block, one, result)
        solved_own[...] = result
        for step in range(2):
            move_start(
                workers[step],
                own_or_none[step],
                solved_own,
                solved.at[agg_rows(core)],
                coarse_send_sem.at[2 + step],
                coarse_recv_sem.at[2 + step],
            )

    def coarse_end():
        for step, side in enumerate(cores):
            wait_bytes(solved.at[agg_rows(side)], coarse_recv_sem.at[2 + step])
            move_sent(own_or_none[step], solved_own, coarse_send_sem.at[2 + step])
        spread = dot_exact(group_spread[...], split(solved[...]))
        return dot_split(spread, (modes_t_h[...], modes_t_l[...]))

    def precondition(residual_ref, turn, started, later=None):
        def beside():
            started()
            coarse_solve()

        changed = operate(pre[...], turn, beside)
        pre[...] += (residual_ref[...] - changed) * inv_diag[...]
        changed = operate(pre[...], 1 - turn, later)
        pre[...] += (residual_ref[...] - changed) * inv_diag[...]
        return pre[...] + coarse_end()

    def lanes(left, right):
        total = jnp.sum(left * right, axis=0, keepdims=True)
        tail = jnp.concatenate([total[:, elems:], jnp.zeros((1, rest), F32)], 1)
        return total[:, :elems] + tail

    stage_steps = [
        [step for step in steps if step[2:] == (0, 0)],
        [step for step in steps if step[:2] == (0, 0)],
    ]
    stage_spots = [quarter * PAIR + low, x * 2 + core]
    stage_buffers = [dots_a, dots_b]

    def dots_send(which, stage, row):
        spot = stage_buffers[stage].at[which, stage_spots[stage]]
        spot[...] = row
        for step in stage_steps[stage]:
            pltpu.make_async_remote_copy(
                src_ref=spot,
                dst_ref=spot,
                send_sem=dots_send_sem.at[which, stage],
                recv_sem=dots_recv_sem.at[which, stage],
                device_id=reached(step)[0],
                device_id_type=MESH,
            ).start()

    def dots_sum(which, stage):
        blocks = stage_buffers[stage].at[which, pl.ds(0, len(stage_steps[stage]))]
        wait_bytes(blocks, dots_recv_sem.at[which, stage])
        wait_bytes(blocks, dots_send_sem.at[which, stage])
        return jnp.sum(stage_buffers[stage][which], axis=0)

    def dots_start(which, pieces):
        column = jnp.concatenate(list(pieces) + [jnp.zeros((8 - len(pieces), elems), F32)], 0)
        column = jnp.sum(column, axis=1, keepdims=True)
        across = lax.broadcasted_iota(jnp.int32, (8, elems), 1)
        down = lax.broadcasted_iota(jnp.int32, (8, elems), 0)
        row = jnp.sum(jnp.where(across == down, column, 0.0), axis=0, keepdims=True)
        dots_send(which, 0, row)

    def dots_next(which):
        dots_send(which, 1, dots_sum(which, 0))

    def dots_end(which):
        total = dots_sum(which, 1)
        return [total[:, lane : lane + 1] for lane in range(8)]

    @pl.loop(0, 2)
    def _(solve):
        def first_time():
            @pl.when(solve == 0)
            def _():
                moved_end(2)
                visc[...] = moved[1].T
                moved_end(3)
                fric[...] = moved[2].T
                inv_diag[...] = inverse_diagonal(visc[...], fric[...], count[...])
                start = pre[...] / inv_diag[...]
                probe_sens[...] = start
                rhs[...] = start
                coarse_start(start)
                moved_start(4)

        @pl.when(solve != 0)
        def _():
            coarse_start(rhs[...])

        first_dir[...] = precondition(rhs, 0, first_time)
        image[...] = operate(first_dir[...], 0)
        pre[...] = image[...] * inv_diag[...]
        coarse_start(image[...])

        def sums_first():
            dots_start(
                0, [lanes(rhs[...], first_dir[...]), lanes(first_dir[...], image[...])]
            )

        second = precondition(image, 1, sums_first, functools.partial(dots_next, 0))
        energy_now, curve, *_ = dots_end(0)
        step = energy_now / curve
        second = first_dir[...] - step * second
        residual = rhs[...] - step * image[...]
        pre[...] = second
        energy_second = energy(pre[...], 1)
        second = pre[...]
        dots_start(
            1,
            [
                lanes(residual, second),
                energy_second,
                lanes(second, image[...]),
                lanes(probe_sens[...], first_dir[...]),
                lanes(probe_sens[...], second),
            ],
        )

        @pl.when(solve == 0)
        def _():
            moved_end(4)
            misfit[...] = moved[3].T

        dots_next(1)
        energy_next, curve_zz, curve_zp, trace_first, trace_second, *_ = dots_end(1)
        ratio = energy_next / energy_now
        curve_next = curve_zz + 2.0 * ratio * curve_zp + ratio * ratio * curve
        step_next = energy_next / curve_next
        weight_first = step + step_next * ratio
        result = weight_first * first_dir[...] + step_next * pre[...]
        result_out[solve] = result.T
        move_start(
            homes[0],
            at_home,
            result_out.at[solve],
            result_in.at[solve],
            move_send_sem.at[6 + solve],
            move_recv_sem.at[6 + solve],
        )
        source = misfit[...] * result
        rhs[...] = source
        pre[...] = source * inv_diag[...]
        value = weight_first * trace_first + step_next * trace_second
        traces[...] = jnp.broadcast_to(value, traces.shape)

    traces_all[probe] = traces[...]
    for device in mates:
        pltpu.make_async_remote_copy(
            src_ref=traces,
            dst_ref=traces_all.at[probe],
            send_sem=last_send_sem,
            recv_sem=last_recv_sem,
            device_id=device,
            device_id_type=MESH,
        ).start()
    for solve in range(2):
        wait_bytes(result_in.at[solve], move_recv_sem.at[6 + solve])
        move_sent(at_home, result_out.at[solve], move_send_sem.at[6 + solve])
    first_out[0] = result_in[0]
    second_out[0] = result_in[1] * sens_in[...]
    blocks = traces_all.at[pl.ds(0, probes - 1)]
    wait_bytes(blocks, last_recv_sem)
    wait_bytes(blocks, last_send_sem)
    trace_out[...] = jnp.sum(traces_all[...], axis=0) / probes


def on_device(
    probes,
    viscosity,
    friction,
    sensitivity,
    misfit_weight,
    grad_ref,
    trace_ref,
    coarse_modes,
    coarse_inv,
    peer_slots,
    local_pairs,
    elem_agg,
):
    leaves, aggs, count = (lax.axis_size(axis) for axis in AXES)
    parts = leaves * aggs
    ndof, elems = viscosity.shape
    own_aggs, modes_n = coarse_inv.shape[:2]
    slots = parts * CAP
    ints = jnp.concatenate(
        [
            peer_slots.reshape(slots // elems, elems),
            local_pairs,
            elem_agg[None],
            jnp.zeros((5, elems), jnp.int32),
        ]
    ).astype(F32)

    def vmem(*shape, dtype=F32):
        return pltpu.VMEM(shape, dtype)

    field = vmem(elems, ndof)
    block_rows = CAP + CAP // 2
    dma = pltpu.SemaphoreType.DMA
    scratch = [
        vmem(1, ndof, elems),
        vmem(ndof, elems),
        vmem(ndof, elems),
        vmem(ndof, elems),
        vmem(ndof, ndof),
        vmem(ndof, ndof),
        vmem(ndof, modes_n),
        vmem(own_aggs, modes_n, modes_n),
        vmem(4, ndof, ndof, dtype=BF16),
        vmem(4, ndof, ndof, dtype=BF16),
        vmem(ndof, modes_n, dtype=BF16),
        vmem(ndof, modes_n, dtype=BF16),
        vmem(modes_n, ndof, dtype=BF16),
        vmem(modes_n, ndof, dtype=BF16),
        vmem(own_aggs, modes_n, modes_n, dtype=BF16),
        vmem(own_aggs, modes_n, modes_n, dtype=BF16),
        vmem(elems, slots, dtype=BF16),
        vmem(2 * elems, slots // 2, dtype=BF16),
        vmem(slots, 2 * elems, dtype=BF16),
        vmem(slots // 2, 2 * elems, dtype=BF16),
        vmem(elems, elems, dtype=BF16),
        vmem(aggs * own_aggs, elems, dtype=BF16),
        vmem(elems, elems, dtype=BF16),
        field,
        field,
        field,
        field,
        vmem(elems, 1),
        vmem(elems, 1),
        field,
        field,
        field,
        field,
        field,
        vmem(8, elems),
        vmem(ndof, elems),
        vmem(4, ndof, elems),
        vmem(*ints.shape),
        vmem(2, ndof, elems),
        vmem(2, ndof, elems),
        vmem(2, parts, block_rows, elems),
        vmem(2, parts, block_rows, elems),
        vmem(aggs * own_aggs, modes_n),
        vmem(2, own_aggs, modes_n),
        vmem(own_aggs, modes_n),
        vmem(elems, modes_n),
        vmem(2, count * PAIR, 1, elems),
        vmem(2, 2 * X, 1, elems),
        vmem(count, 8, elems),
        dma((2,)),
        dma((2,)),
        dma((8,)),
        dma((8,)),
        dma((4,)),
        dma((4,)),
        dma((2, 2)),
        dma((2, 2)),
        dma,
        dma,
        dma((8,)),
    ]
    field_out = jax.ShapeDtypeStruct((1, ndof, elems), F32)
    first, second, trace_tile = pl.pallas_call(
        functools.partial(kernel, parts, count),
        out_shape=(
            field_out,
            field_out,
            jax.ShapeDtypeStruct((8, elems), F32),
        ),
        in_specs=[pl.BlockSpec(memory_space=pltpu.HBM)] * 9
        + [pl.BlockSpec(memory_space=pltpu.VMEM)],
        out_specs=(pl.BlockSpec(memory_space=pltpu.VMEM),) * 3,
        scratch_shapes=scratch,
        compiler_params=pltpu.CompilerParams(
            collective_id=0, has_side_effects=True, vmem_limit_bytes=60 * 1024 * 1024
        ),
    )(
        probes,
        viscosity,
        friction,
        sensitivity,
        misfit_weight,
        grad_ref,
        trace_ref,
        coarse_modes,
        coarse_inv,
        ints,
    )
    return first, second, trace_tile[0, 0]


def solution(mesh):
    in_specs = (
        P("probe", None, ("leaf", "agg")),
        P(None, ("leaf", "agg")),
        P(None, ("leaf", "agg")),
        P(None, ("leaf", "agg")),
        P(None, ("leaf", "agg")),
        P(),
        P(),
        P(),
        P(("leaf", "agg"), None, None),
        P(("leaf", "agg"), None, None),
        P(None, ("leaf", "agg")),
        P(("leaf", "agg")),
    )
    out_specs = (P("probe", None, ("leaf", "agg")), P("probe", None, ("leaf", "agg")), P())
    return jax.shard_map(
        on_device, mesh=mesh, in_specs=in_specs, out_specs=out_specs, check_vma=False
    )
```

```python
import functools
import jax
import jax.numpy as jnp
from jax import lax
from jax.experimental import pallas as pl
from jax.experimental.pallas import tpu as pltpu
from jax.sharding import PartitionSpec as P

MESH = pl.DeviceIdType.MESH
F32 = jnp.float32
BF16 = jnp.bfloat16
AXES = ("leaf", "agg", "probe")
RELAX = 0.6
CAP = 16
NT = (((1,), (1,)), ((), ()))
X = 4

PAIR = 2


def split(value):
    high = value.astype(BF16)
    return high, (value - high.astype(F32)).astype(BF16)


def dot(left, right):
    return jnp.dot(left, right, preferred_element_type=F32)


def dot_exact(left, right_pair):
    return dot(left, right_pair[0]) + dot(left, right_pair[1])


def dot_wide(left, right):
    width = right.shape[1]
    both = dot(left, jnp.concatenate(split(right), 1))
    return both[:, :width] + both[:, width:]


def dot_split(left, right_pair):
    left_high, left_low = split(left)
    return dot(left_high, right_pair[0]) + (
        dot(left_low, right_pair[0]) + dot(left_high, right_pair[1])
    )


def group_steps(probes):
    def hops(step):
        return -(min(step[0], probes - step[0]) + step[1] + min(step[2], X - step[2]))

    steps = [
        (y, z, x, core)
        for y in range(probes)
        for z in range(PAIR)
        for x in range(X)
        for core in range(2)
    ][1:]
    return sorted(steps, key=hops)


def kernel(
    parts,
    probes,
    probe_far,
    visc_far,
    fric_far,
    sens_far,
    misfit_far,
    grad_far,
    trace_far,
    modes_far,
    inv_far,
    ints_in,
    out,
    trace_out,
    probe_in,
    visc_in,
    fric_in,
    sens_in,
    grad,
    trace,
    modes,
    inv,
    weights_h,
    weights_l,
    modes_h,
    modes_l,
    modes_t_h,
    modes_t_l,
    inv_h,
    inv_l,
    scatter,
    scatter_two,
    gather,
    gather_two,
    adjacent,
    group_sum,
    group_spread,
    visc,
    fric,
    misfit,
    inv_diag,
    count,
    count_near,
    probe_sens,
    rhs,
    first_dir,
    image,
    pre,
    traces,
    home,
    moved,
    ints,
    result_out,
    result_in,
    send,
    recv,
    sums,
    sums_in,
    solved_own,
    solved,
    dots_a,
    dots_b,
    traces_all,
    send_sem,
    recv_sem,
    move_send_sem,
    move_recv_sem,
    coarse_send_sem,
    coarse_recv_sem,
    dots_send_sem,
    dots_recv_sem,
    last_send_sem,
    last_recv_sem,
    load_sem,
):
    loads = [
        pltpu.make_async_copy(far, near, load_sem.at[which])
        for which, (far, near) in enumerate(
            [
                (visc_far, visc_in),
                (grad_far, grad),
                (fric_far, fric_in),
                (trace_far, trace),
                (sens_far, sens_in),
                (probe_far, probe_in),
                (modes_far, modes),
                (inv_far, inv),
            ]
        )
    ]
    for load in loads:
        load.start()
    leaf, core, along = lax.axis_index("leaf"), lax.axis_index("agg"), lax.axis_index("probe")
    z, x = lax.div(leaf, X), lax.rem(leaf, X)
    probe, low = lax.div(z, PAIR), lax.rem(z, PAIR)
    quarter = lax.rem(along - probe + probes, probes)
    unit = ((quarter * PAIR + low) * X + x) * 2 + core
    at_home = along + probe == 0
    in_place = quarter == probe
    ndof = grad.shape[0]
    elems = visc_in.shape[1]
    slots = parts * CAP
    halves = CAP // 2
    others = parts - 1
    rest = 2 * elems - ndof

    lows = [lax.rem(low + step, PAIR) for step in range(PAIR)]
    xs = [lax.rem(x + step, X) for step in range(X)]
    cores = [core, 1 - core]
    alongs = [lax.rem(along + step, probes) for step in range(probes)]
    quarters = [lax.rem(quarter + step, probes) for step in range(probes)]
    leaves = [[(probe * PAIR + part) * X + place for place in xs] for part in lows]

    def reached(step):
        y_step, z_step, x_step, core_step = step
        device = (leaves[z_step][x_step], cores[core_step], alongs[y_step])
        peer = (quarters[y_step] * PAIR + lows[z_step]) * X + xs[x_step]
        peer = peer * 2 + cores[core_step]
        return device, peer

    steps = group_steps(probes)
    peers = [reached(step) for step in steps]
    inverse = {
        step: ((probes - step[0]) % probes, step[1], (X - step[2]) % X, step[3]) for step in steps
    }
    pair_steps = [
        step
        for step in steps
        if step == inverse[step]
        or (step < inverse[step]) == ((step[1] + step[3]) % 2 == 0)
    ]
    mates = [
        ((lax.rem(probe + step, probes) * PAIR + low) * X + x, core, along)
        for step in range(1, probes)
    ]
    away = (quarter * PAIR + low) * X + x
    homes = [(away, side, probe) for side in cores]
    workers = [
        ((along * PAIR + low) * X + x, side, lax.rem(probe + along, probes)) for side in cores
    ]
    plane = (away, core, along)

    barrier = pltpu.get_barrier_semaphore()
    for device in [device for device, _ in peers] + mates:
        pl.semaphore_signal(barrier, inc=1, device_id=device, device_id_type=MESH)

    @pl.when(jnp.logical_not(at_home))
    def _():
        for device in homes + workers:
            pl.semaphore_signal(barrier, inc=1, device_id=device, device_id_type=MESH)

    @pl.when(jnp.logical_not(in_place))
    def _():
        pl.semaphore_signal(barrier, inc=1, device_id=plane, device_id_type=MESH)

    def wait_bytes(ref, sem):
        pltpu.make_async_copy(ref, ref, sem).wait()

    def move_start(device, stays, source, target, send_at, recv_at):
        def remote():
            pltpu.make_async_remote_copy(
                src_ref=source,
                dst_ref=target,
                send_sem=send_at,
                recv_sem=recv_at,
                device_id=device,
                device_id_type=MESH,
            ).start()

        if stays is None:
            remote()
        else:

            @pl.when(stays)
            def _():
                pltpu.make_async_copy(source, target, recv_at).start()

            @pl.when(jnp.logical_not(stays))
            def _():
                remote()

    def move_sent(stays, source, send_at):
        if stays is None:
            wait_bytes(source, send_at)
        else:

            @pl.when(jnp.logical_not(stays))
            def _():
                wait_bytes(source, send_at)

    own_or_none = [at_home, None]

    rows = lax.broadcasted_iota(jnp.int32, (elems, elems), 0).astype(F32)

    def one_hot(ref, row):
        return (ref[pl.ds(row, 1), :] == rows).astype(F32)

    base = slots // elems

    def adjacency(ref):
        ends = [one_hot(ref, base + end).astype(BF16) for end in range(2)]
        near = lax.dot_general(ends[0], ends[1], NT, preferred_element_type=F32)
        return near + lax.dot_general(ends[1], ends[0], NT, preferred_element_type=F32)

    def inverse_diagonal(visc_t, fric_t, counts):
        square = grad[...] * grad[...]
        trace_square = jnp.sum(trace[...] * trace[...], axis=0, keepdims=True)
        return RELAX / (dot_split(visc_t, split(square)) + fric_t + counts * trace_square)

    touching = jnp.zeros((elems, 1), F32)
    for block in range(base):
        touching = touching + jnp.sum(one_hot(ints_in, block), axis=1, keepdims=True)
    touching = touching + jnp.sum(adjacency(ints_in), axis=1, keepdims=True)
    for load in loads[:6]:
        load.wait()
    home_diag = inverse_diagonal(visc_in[...].T, fric_in[...].T, touching)
    home[...] = ((sens_in[...] * probe_in[0]).T * home_diag).T
    for turn in range(2):
        recv[turn, unit] = jnp.zeros(recv.shape[2:], F32)

    @pl.when(at_home)
    def _():
        pl.semaphore_wait(barrier, others + probes - 1)

    @pl.when(jnp.logical_and(in_place, jnp.logical_not(at_home)))
    def _():
        pl.semaphore_wait(barrier, others + probes + 3)

    @pl.when(jnp.logical_not(in_place))
    def _():
        pl.semaphore_wait(barrier, others + probes + 4)

    sources = [ints_in, home, visc_in, fric_in, misfit_far]
    targets = [ints] + [moved.at[which] for which in range(4)]

    ways = [(plane, in_place), (workers[0], at_home)] + [(plane, in_place)] * 3

    def moved_start(which):
        device, stays = ways[which]
        move_start(
            device,
            stays,
            sources[which],
            targets[which],
            move_send_sem.at[which],
            move_recv_sem.at[which],
        )

    def moved_end(which):
        wait_bytes(targets[which], move_recv_sem.at[which])
        move_sent(ways[which][1], sources[which], move_send_sem.at[which])

    for which in range(4):
        moved_start(which)

    for slot, matrix in enumerate((grad[...].T, grad[...], trace[...].T, trace[...])):
        weights_h[slot], weights_l[slot] = split(matrix)
    for load in loads[6:]:
        load.wait()
    modes_h[...], modes_l[...] = split(modes[...])
    modes_t_h[...], modes_t_l[...] = split(modes[...].T)
    for block in range(inv.shape[0]):
        inv_h[block], inv_l[block] = split(inv[block])
    moved_end(0)
    cross = jnp.zeros((elems, 1), F32)
    for block in range(base):
        hot = one_hot(ints, block)
        cross = cross + jnp.sum(hot, axis=1, keepdims=True)
        here = pl.ds(block * elems, elems)
        scatter[:, here] = hot.astype(BF16)
        hot_t = hot.T
        gather[here, :elems] = hot_t.astype(BF16)
        gather[here, elems:] = hot_t.astype(BF16)
        paired = hot_t.reshape(elems // CAP, 2, halves, elems)
        half = pl.ds(block * (elems // 2), elems // 2)
        gather_two[half, :elems] = paired[:, 0].reshape(elems // 2, elems).astype(BF16)
        gather_two[half, elems:] = paired[:, 1].reshape(elems // 2, elems).astype(BF16)
    for block in range(base // 2):
        here = pl.ds(block * elems, elems)
        scatter_two[:elems, here] = gather_two[here, :elems].astype(F32).T.astype(BF16)
        scatter_two[elems:, here] = gather_two[here, elems:].astype(F32).T.astype(BF16)
    near_pairs = adjacency(ints)
    adjacent[...] = near_pairs.astype(BF16)
    count_near[...] = jnp.sum(near_pairs, axis=1, keepdims=True)
    count[...] = cross + count_near[...]
    hot = one_hot(ints, base + 2)
    group_sum[...] = hot[: sums.shape[0]].astype(BF16)
    group_spread[...] = hot.T.astype(BF16)
    solved[...] = jnp.zeros_like(solved)
    moved_end(1)
    pre[...] = moved[0].T

    def weight(slot):
        return weights_h[slot], weights_l[slot]

    def wait_blocks(turn, sem, blocks=others):
        wait_bytes(recv.at[turn, pl.ds(0, blocks)], sem.at[turn])

    def send_traces(value, turn, receivers):
        traced = dot_split(value, weight(2))
        high, low_part = split(traced)
        blank = jnp.zeros((elems, rest), BF16)
        both = jnp.concatenate([high[:, :elems], low_part[:, :elems]], 0)
        send[turn, :, :CAP, :] = dot(gather[...], both).reshape(parts, CAP, elems)

        def two(piece):
            tail = piece[:, elems:]
            return jnp.concatenate(
                [jnp.concatenate([tail, blank], 1), jnp.concatenate([blank, tail], 1)], 0
            )

        send[turn, :, CAP:, :] = dot_exact(
            gather_two[...], (two(high), two(low_part))
        ).reshape(parts, halves, elems)
        for device, peer in receivers:
            pltpu.make_async_remote_copy(
                src_ref=send.at[turn, peer],
                dst_ref=recv.at[turn, unit],
                send_sem=send_sem.at[turn],
                recv_sem=recv_sem.at[turn],
                device_id=device,
                device_id_type=MESH,
            ).start()
        return traced, high, low_part

    def energy(value, turn):
        traced, high, low_part = send_traces(value, turn, [reached(step) for step in pair_steps])
        strain = dot_split(value, weight(0))
        near = count_near[...] * traced - dot_exact(adjacent[...], (high, low_part))
        total = lanes(visc[...] * strain, strain)
        total = total + lanes(fric[...] * value, value) + lanes(near, traced)
        wait_blocks(turn, recv_sem, len(pair_steps))
        once = jnp.zeros(recv.shape[2:], F32)
        twice = jnp.zeros(recv.shape[2:], F32)
        for step in pair_steps:
            _, peer = reached(inverse[step])
            jump = send[turn, peer] - recv[turn, peer]
            if step == inverse[step]:
                twice = twice + jump * jump
            else:
                once = once + jump * jump
        wait_blocks(turn, send_sem, len(pair_steps))
        return total + jnp.sum(once + 0.5 * twice, axis=0, keepdims=True)

    def operate(value, turn, started=None):
        traced, high, low_part = send_traces(value, turn, peers)
        if started is not None:
            started()
        inner = dot_split(visc[...] * dot_split(value, weight(0)), weight(1))
        near = count[...] * traced - dot_exact(adjacent[...], (high, low_part))
        inner = inner + fric[...] * value
        wait_blocks(turn, recv_sem)
        first = dot_wide(scatter[...], recv[turn, :, :CAP, :].reshape(slots, elems))
        second = dot_wide(scatter_two[...], recv[turn, :, CAP:, :].reshape(slots // 2, elems))
        second = second[:elems, :rest] + second[elems:, rest:]
        near = near - jnp.concatenate([first, second], 1)
        result = inner + dot_split(near, weight(3))
        wait_blocks(turn, send_sem)
        return result

    own_aggs = inv.shape[0]

    def agg_rows(side):
        return pl.ds(pl.multiple_of(side * own_aggs, own_aggs), own_aggs)

    def coarse_start(residual):
        projected = dot_split(residual, (modes_h[...], modes_l[...]))
        sums[...] = dot_exact(group_sum[...], split(projected))
        for step, side in enumerate(cores):
            move_start(
                homes[step],
                own_or_none[step],
                sums.at[agg_rows(side)],
                sums_in.at[step],
                coarse_send_sem.at[step],
                coarse_recv_sem.at[step],
            )

    def coarse_solve():
        for step, side in enumerate(cores):
            wait_bytes(sums_in.at[step], coarse_recv_sem.at[step])
            move_sent(own_or_none[step], sums.at[agg_rows(side)], coarse_send_sem.at[step])
        total = sums_in[0] + sums_in[1]
        row = lax.broadcasted_iota(jnp.int32, total.shape, 0)
        result = jnp.zeros_like(total)
        for block in range(own_aggs):
            one = dot_split(total, (inv_h[block], inv_l[block]))
            result = jnp.where(row == block, one, result)
        solved_own[...] = result
        for step in range(2):
            move_start(
                workers[step],
                own_or_none[step],
                solved_own,
                solved.at[agg_rows(core)],
                coarse_send_sem.at[2 + step],
                coarse_recv_sem.at[2 + step],
            )

    def coarse_end():
        for step, side in enumerate(cores):
            wait_bytes(solved.at[agg_rows(side)], coarse_recv_sem.at[2 + step])
            move_sent(own_or_none[step], solved_own, coarse_send_sem.at[2 + step])
        spread = dot_exact(group_spread[...], split(solved[...]))
        return dot_split(spread, (modes_t_h[...], modes_t_l[...]))

    def precondition(residual_ref, turn, started, later=None):
        def beside():
            started()
            coarse_solve()

        changed = operate(pre[...], turn, beside)
        pre[...] += (residual_ref[...] - changed) * inv_diag[...]
        changed = operate(pre[...], 1 - turn, later)
        pre[...] += (residual_ref[...] - changed) * inv_diag[...]
        return pre[...] + coarse_end()

    def lanes(left, right):
        total = jnp.sum(left * right, axis=0, keepdims=True)
        tail = jnp.concatenate([total[:, elems:], jnp.zeros((1, rest), F32)], 1)
        return total[:, :elems] + tail

    stage_steps = [
        [step for step in steps if step[2:] == (0, 0)],
        [step for step in steps if step[:2] == (0, 0)],
    ]
    stage_spots = [quarter * PAIR + low, x * 2 + core]
    stage_buffers = [dots_a, dots_b]

    def dots_send(which, stage, row):
        spot = stage_buffers[stage].at[which, stage_spots[stage]]
        spot[...] = row
        for step in stage_steps[stage]:
            pltpu.make_async_remote_copy(
                src_ref=spot,
                dst_ref=spot,
                send_sem=dots_send_sem.at[which, stage],
                recv_sem=dots_recv_sem.at[which, stage],
                device_id=reached(step)[0],
                device_id_type=MESH,
            ).start()

    def dots_sum(which, stage):
        blocks = stage_buffers[stage].at[which, pl.ds(0, len(stage_steps[stage]))]
        wait_bytes(blocks, dots_recv_sem.at[which, stage])
        wait_bytes(blocks, dots_send_sem.at[which, stage])
        return jnp.sum(stage_buffers[stage][which], axis=0)

    def dots_start(which, pieces):
        column = jnp.concatenate(list(pieces) + [jnp.zeros((8 - len(pieces), elems), F32)], 0)
        column = jnp.sum(column, axis=1, keepdims=True)
        across = lax.broadcasted_iota(jnp.int32, (8, elems), 1)
        down = lax.broadcasted_iota(jnp.int32, (8, elems), 0)
        row = jnp.sum(jnp.where(across == down, column, 0.0), axis=0, keepdims=True)
        dots_send(which, 0, row)

    def dots_next(which):
        dots_send(which, 1, dots_sum(which, 0))

    def dots_end(which):
        total = dots_sum(which, 1)
        return [total[:, lane : lane + 1] for lane in range(8)]

    @pl.loop(0, 2)
    def _(solve):
        def first_time():
            @pl.when(solve == 0)
            def _():
                moved_end(2)
                visc[...] = moved[1].T
                moved_end(3)
                fric[...] = moved[2].T
                inv_diag[...] = inverse_diagonal(visc[...], fric[...], count[...])
                start = pre[...] / inv_diag[...]
                probe_sens[...] = start
                rhs[...] = start
                coarse_start(start)
                moved_start(4)

        @pl.when(solve != 0)
        def _():
            coarse_start(rhs[...])

        first_dir[...] = precondition(rhs, 0, first_time)
        image[...] = operate(first_dir[...], 0)
        pre[...] = image[...] * inv_diag[...]
        coarse_start(image[...])

        def sums_first():
            dots_start(
                0, [lanes(rhs[...], first_dir[...]), lanes(first_dir[...], image[...])]
            )

        second = precondition(image, 1, sums_first, functools.partial(dots_next, 0))
        energy_now, curve, *_ = dots_end(0)
        step = energy_now / curve
        second = first_dir[...] - step * second
        residual = rhs[...] - step * image[...]
        pre[...] = second
        energy_second = energy(pre[...], 1)
        second = pre[...]
        dots_start(
            1,
            [
                lanes(residual, second),
                energy_second,
                lanes(second, image[...]),
                lanes(probe_sens[...], first_dir[...]),
                lanes(probe_sens[...], second),
            ],
        )

        @pl.when(solve == 0)
        def _():
            moved_end(4)
            misfit[...] = moved[3].T

        dots_next(1)
        energy_next, curve_zz, curve_zp, trace_first, trace_second, *_ = dots_end(1)
        ratio = energy_next / energy_now
        curve_next = curve_zz + 2.0 * ratio * curve_zp + ratio * ratio * curve
        step_next = energy_next / curve_next
        weight_first = step + step_next * ratio
        result = weight_first * first_dir[...] + step_next * pre[...]
        result_out[solve] = result.T
        move_start(
            homes[0],
            at_home,
            result_out.at[solve],
            result_in.at[solve],
            move_send_sem.at[6 + solve],
            move_recv_sem.at[6 + solve],
        )
        source = misfit[...] * result
        rhs[...] = source
        pre[...] = source * inv_diag[...]
        value = weight_first * trace_first + step_next * trace_second
        traces[...] = jnp.broadcast_to(value, traces.shape)

    traces_all[probe] = traces[...]
    for device in mates:
        pltpu.make_async_remote_copy(
            src_ref=traces,
            dst_ref=traces_all.at[probe],
            send_sem=last_send_sem,
            recv_sem=last_recv_sem,
            device_id=device,
            device_id_type=MESH,
        ).start()
    for solve in range(2):
        wait_bytes(result_in.at[solve], move_recv_sem.at[6 + solve])
        move_sent(at_home, result_out.at[solve], move_send_sem.at[6 + solve])
    out[0] = result_in[0]
    out[1] = result_in[1] * sens_in[...]
    blocks = traces_all.at[pl.ds(0, probes - 1)]
    wait_bytes(blocks, last_recv_sem)
    wait_bytes(blocks, last_send_sem)
    trace_out[...] = jnp.sum(traces_all[...], axis=0) / probes


def on_device(
    probes,
    viscosity,
    friction,
    sensitivity,
    misfit_weight,
    grad_ref,
    trace_ref,
    coarse_modes,
    coarse_inv,
    peer_slots,
    local_pairs,
    elem_agg,
):
    leaves, aggs, count = (lax.axis_size(axis) for axis in AXES)
    parts = leaves * aggs
    ndof, elems = viscosity.shape
    own_aggs, modes_n = coarse_inv.shape[:2]
    slots = parts * CAP
    ints = jnp.concatenate(
        [
            peer_slots.reshape(slots // elems, elems),
            local_pairs,
            elem_agg[None],
            jnp.zeros((5, elems), jnp.int32),
        ]
    ).astype(F32)

    def vmem(*shape, dtype=F32):
        return pltpu.VMEM(shape, dtype)

    field = vmem(elems, ndof)
    block_rows = CAP + CAP // 2
    dma = pltpu.SemaphoreType.DMA
    scratch = [
        vmem(1, ndof, elems),
        vmem(ndof, elems),
        vmem(ndof, elems),
        vmem(ndof, elems),
        vmem(ndof, ndof),
        vmem(ndof, ndof),
        vmem(ndof, modes_n),
        vmem(own_aggs, modes_n, modes_n),
        vmem(4, ndof, ndof, dtype=BF16),
        vmem(4, ndof, ndof, dtype=BF16),
        vmem(ndof, modes_n, dtype=BF16),
        vmem(ndof, modes_n, dtype=BF16),
        vmem(modes_n, ndof, dtype=BF16),
        vmem(modes_n, ndof, dtype=BF16),
        vmem(own_aggs, modes_n, modes_n, dtype=BF16),
        vmem(own_aggs, modes_n, modes_n, dtype=BF16),
        vmem(elems, slots, dtype=BF16),
        vmem(2 * elems, slots // 2, dtype=BF16),
        vmem(slots, 2 * elems, dtype=BF16),
        vmem(slots // 2, 2 * elems, dtype=BF16),
        vmem(elems, elems, dtype=BF16),
        vmem(aggs * own_aggs, elems, dtype=BF16),
        vmem(elems, elems, dtype=BF16),
        field,
        field,
        field,
        field,
        vmem(elems, 1),
        vmem(elems, 1),
        field,
        field,
        field,
        field,
        field,
        vmem(8, elems),
        vmem(ndof, elems),
        vmem(4, ndof, elems),
        vmem(*ints.shape),
        vmem(2, ndof, elems),
        vmem(2, ndof, elems),
        vmem(2, parts, block_rows, elems),
        vmem(2, parts, block_rows, elems),
        vmem(aggs * own_aggs, modes_n),
        vmem(2, own_aggs, modes_n),
        vmem(own_aggs, modes_n),
        vmem(elems, modes_n),
        vmem(2, count * PAIR, 1, elems),
        vmem(2, 2 * X, 1, elems),
        vmem(count, 8, elems),
        dma((2,)),
        dma((2,)),
        dma((8,)),
        dma((8,)),
        dma((4,)),
        dma((4,)),
        dma((2, 2)),
        dma((2, 2)),
        dma,
        dma,
        dma((8,)),
    ]
    out, trace_tile = pl.pallas_call(
        functools.partial(kernel, parts, count),
        out_shape=(
            jax.ShapeDtypeStruct((2, ndof, elems), F32),
            jax.ShapeDtypeStruct((8, elems), F32),
        ),
        in_specs=[pl.BlockSpec(memory_space=pltpu.HBM)] * 9
        + [pl.BlockSpec(memory_space=pltpu.VMEM)],
        out_specs=(pl.BlockSpec(memory_space=pltpu.VMEM),) * 2,
        scratch_shapes=scratch,
        compiler_params=pltpu.CompilerParams(
            collective_id=0, has_side_effects=True, vmem_limit_bytes=60 * 1024 * 1024
        ),
    )(
        probes,
        viscosity,
        friction,
        sensitivity,
        misfit_weight,
        grad_ref,
        trace_ref,
        coarse_modes,
        coarse_inv,
        ints,
    )
    return out[0][None], out[1][None], trace_tile[0, 0]


def solution(mesh):
    in_specs = (
        P("probe", None, ("leaf", "agg")),
        P(None, ("leaf", "agg")),
        P(None, ("leaf", "agg")),
        P(None, ("leaf", "agg")),
        P(None, ("leaf", "agg")),
        P(),
        P(),
        P(),
        P(("leaf", "agg"), None, None),
        P(("leaf", "agg"), None, None),
        P(None, ("leaf", "agg")),
        P(("leaf", "agg")),
    )
    out_specs = (P("probe", None, ("leaf", "agg")), P("probe", None, ("leaf", "agg")), P())
    return jax.shard_map(
        on_device, mesh=mesh, in_specs=in_specs, out_specs=out_specs, check_vma=False
    )
```
